32 devices in a mesh: groups: 2 (over y), expert: 4 (over z), tensor: 4 (over x, core).
Axes of the slice: x: 2, y: 2, z: 4, core: 2. Of those that a mesh axis runs over, the one named last changes fastest.
Arguments:
- tokens: bfloat16 [640, 6144], P(('groups', 'expert'), 'tensor'), parts along dimension 0, may hold values from -6 to 6
- expert_ids: int32 [640, 4], P(('groups', 'expert')), parts along dimension 0, may hold values from 0 to 15, as said below
- route_weights: float32 [640, 4], P(('groups', 'expert')), parts along dimension 0, may hold values from 0.1 to 1
- w_gate: bfloat16 [6144, 32768], P(None, ('expert', 'tensor')), may hold values from -0.078125 to 0.078125
- w_up: bfloat16 [6144, 32768], P(None, ('expert', 'tensor')), may hold values from -0.078125 to 0.078125
- w_down: bfloat16 [32768, 6144], P(('expert', 'tensor')), may hold values from -0.0625 to 0.0625
Outputs:
- moe_output: bfloat16 [640, 6144], P(('groups', 'expert'), 'tensor'), parts along dimension 0
The draws below stay inside these ranges and needn't reach their ends.
There are 2 independent parts, one for each index of `groups`. The reference program is written for one: setup_inputs(seed, part) draws one part's arguments, and reference() takes and returns one part's arrays. A program takes and returns all parts, laid end to end along the dimension named above; an argument that names none is the same for every part. Nothing has to cross between parts.
Inputs may be any that keep to these rules, and one draw needn't show every extreme that they name: `expert_ids`: each token names 4 different experts. In each block of 80 tokens in order (the tokens of one index of expert), each expert below 4 is named by at most 10 tokens, and one of them by exactly 10.
All inputs are finite; a program needn't handle non-finite values.
Results may differ from the reference program's by a relative error of at most 0.012.
Values may be sent and summed in bfloat16 or wider, within the bound.
No kernel may reach another device: no remote copies, remote signals or barrier semaphores. Data moves between devices by JAX's collectives and lax.ppermute only.
A program may use at most 192 MiB of HBM per device.

```python
import jax
import jax.numpy as jnp
from jax import lax

D = 6144
EXPERTS = 16
TOP = 4
E_W = 4
FF_W = 8192
SLOT = 10
TOK_DEV = 80
TOKENS = 320
HID_DEV = 2048
N_EXPERT = 4
N_TENSOR = 4


def draw_expert_ids(key, part):
    key = jax.random.fold_in(key, 11)
    blocks = TOKENS // TOK_DEV
    key_counts, key_full, key_order, key_other = jax.random.split(key, 4)
    counts = jax.random.randint(key_counts, (blocks, E_W), (SLOT + 1) // 2, SLOT + 1)
    full_one = jax.random.randint(key_full, (blocks,), 0, E_W)
    counts = jnp.where(jnp.arange(E_W)[None, :] == full_one[:, None], SLOT, counts)
    scores = jax.random.randint(key_order, (blocks, E_W, TOK_DEV), 0, 1 << 20) * TOK_DEV + jnp.arange(TOK_DEV)[None, None, :]
    ordering = jnp.argsort(scores, axis=-1)
    ranking = jnp.argsort(ordering, axis=-1)
    chosen = ranking < counts[:, :, None]
    chosen = jnp.transpose(chosen, (0, 2, 1)).reshape(TOKENS, E_W)
    others = jax.random.randint(key_other, (TOKENS, EXPERTS - E_W), 0, 1 << 16) * EXPERTS + jnp.arange(E_W, EXPERTS)[None, :]
    window_scores = jnp.where(chosen, (1 << 24) + jnp.arange(E_W)[None, :], -1 - jnp.arange(E_W)[None, :])
    combined = jnp.concatenate([window_scores, others], axis=1)
    top_values, chosen_ids = lax.top_k(combined, TOP)
    return chosen_ids.astype(jnp.int32)


def block_scale(stream_key, shape, cuts, least, top_value):
    gain = 1.0
    for axis_at, shards_of in cuts:
        draws = jax.random.uniform(jax.random.fold_in(jax.random.fold_in(stream_key, 6), axis_at), (shards_of,), jnp.float32, least / len(cuts), top_value / len(cuts))
        gain = gain * jnp.repeat(jnp.exp(draws), shape[axis_at] // shards_of).reshape((-1,) + (1,) * (len(shape) - 1 - axis_at))
    return gain


def centred(own_key, extent, width, reach, cuts=(), kind=jnp.bfloat16):
    values = jax.random.normal(own_key, extent, jnp.float32) * width
    if len(cuts) > 0:
        values = block_scale(own_key, extent, cuts, -0.22, 0.18) * values
    return jnp.clip(values, min=-reach, max=reach).astype(kind)


def setup_inputs(seed: int = 0, part: int = 0) -> dict:
    splits = jax.random.split(jax.random.key(seed), 7)
    part_splits = jax.random.split(jax.random.fold_in(splits[6], part), 7)
    return {
        "tokens": centred(part_splits[0], (TOKENS, D), 1.0, 6.0, ((0, 4), (1, 4))),
        "expert_ids": draw_expert_ids(jax.random.fold_in(jax.random.fold_in(splits[6], part), 71), part),
        "route_weights": jnp.clip(0.1 + 0.9 * jax.random.uniform(part_splits[2], (TOKENS, TOP), jnp.float32) ** block_scale(part_splits[2], (TOKENS, TOP), ((0, 4),), -0.2, 0.2), 0.1, 1.0),
        "w_gate": centred(splits[3], (D, E_W * FF_W), D ** -0.5, 0.078125, ((1, 16),)),
        "w_up": centred(splits[4], (D, E_W * FF_W), D ** -0.5, 0.078125, ((1, 16),)),
        "w_down": centred(splits[5], (E_W * FF_W, D), FF_W ** -0.5, 0.0625, ((0, 16),)),
    }


def reference(tokens, expert_ids, route_weights, w_gate, w_up, w_down):
    blocks = TOKENS // TOK_DEV
    replicas = N_EXPERT // E_W
    picked = expert_ids[:, :, None] == jnp.arange(E_W, dtype=jnp.int32)[None, None, :]
    weight_e = jnp.sum(jnp.where(picked, route_weights[:, :, None], jnp.float32(0.0)), axis=1)
    member = jnp.any(picked, axis=1).reshape(blocks, TOK_DEV, E_W)
    position = jnp.cumsum(member.astype(jnp.int32), axis=1) - 1
    token_index = jnp.arange(TOKENS, dtype=jnp.int32).reshape(blocks, TOK_DEV)
    padded = jnp.concatenate([tokens, jnp.zeros((1, D), tokens.dtype)], axis=0)
    accumulated = jnp.zeros((TOKENS, D), jnp.float32)
    row_count = blocks * SLOT
    for expert_no in range(E_W):
        slot_of = jnp.where(member[:, :, expert_no], position[:, :, expert_no], SLOT).astype(jnp.int32)
        slot_table = jnp.full((blocks, SLOT + 1), TOKENS, jnp.int32)
        slot_table = slot_table.at[jnp.arange(blocks, dtype=jnp.int32)[:, None], slot_of].set(token_index)
        row_index = slot_table[:, :SLOT].reshape(-1)
        gathered_rows = padded[row_index]
        first = expert_no * FF_W
        gate_proj = jnp.dot(gathered_rows, w_gate[:, first:first + FF_W], preferred_element_type=jnp.float32)
        up_proj = jnp.dot(gathered_rows, w_up[:, first:first + FF_W], preferred_element_type=jnp.float32)
        hidden = (jax.nn.silu(gate_proj) * up_proj).astype(jnp.bfloat16)
        hidden_blocks = hidden.reshape(row_count, replicas, N_TENSOR, HID_DEV).transpose(1, 0, 2, 3)
        down_blocks = w_down[first:first + FF_W].reshape(replicas, N_TENSOR, HID_DEV, D)

        def sub_block(operands):
            hidden_part, down_part = operands
            partials = jnp.einsum('rqh,qhd->qrd', hidden_part.astype(jnp.float32), down_part.astype(jnp.float32), precision=lax.Precision.HIGHEST)
            partials = lax.optimization_barrier(partials.astype(jnp.bfloat16)).astype(jnp.float32)
            return jnp.sum(partials, axis=0).astype(jnp.bfloat16)

        sub_sums = lax.map(sub_block, (hidden_blocks, down_blocks))
        expert_out = jnp.sum(sub_sums.astype(jnp.float32), axis=0)
        scattered = jnp.zeros((TOKENS, D), jnp.float32).at[row_index].add(expert_out, mode='drop')
        accumulated = accumulated + weight_e[:, expert_no:expert_no + 1] * scattered
    return accumulated.astype(jnp.bfloat16)
```

```python
import functools

import jax
import jax.numpy as jnp
from jax import lax
from jax.experimental import pallas as pl
from jax.experimental.pallas import tpu as pltpu
from jax.sharding import PartitionSpec as P

E_W = 4
SLOT = 10
SLAB = 16
AHEAD0 = 2
AHEAD1 = 2
WINDOW = 3
MIB = 1 << 20
VMEM = pltpu.VMEM
HBM = pltpu.HBM


def spec(space):
    return pl.BlockSpec(memory_space=space)


def dot(a, b, dims=(((1,), (0,)), ((), ()))):
    return lax.dot_general(a, b, dims, preferred_element_type=jnp.float32)


def iota(shape, dim):
    return lax.broadcasted_iota(jnp.int32, shape, dim)


def select_kernel(n, ids_ref, route_ref, tok_ref, comb_ref, *slabs):
    me = lax.axis_index("expert")
    replicas = n // E_W
    ids, route, tok = ids_ref[...], route_ref[...], tok_ref[...]
    count = tok.shape[0]
    before = (iota((count, count), 0) <= iota((count, count), 1)).astype(jnp.bfloat16)
    slot = iota((SLAB, count), 0).astype(jnp.float32)
    for k in range(n):
        hit = ids == (me ^ k) // replicas
        member = jnp.sum(jnp.where(hit, 1.0, 0.0), axis=0, keepdims=True)
        weight = jnp.sum(jnp.where(hit, route, 0.0), axis=0, keepdims=True)
        member = jnp.broadcast_to(member, (SLAB, count))
        position = dot(member.astype(jnp.bfloat16), before) - 1.0
        placed = jnp.where(position == slot, member, 0.0)
        slabs[k][...] = dot(placed.astype(jnp.bfloat16), tok).astype(jnp.bfloat16)
        comb_ref[k * SLAB : (k + 1) * SLAB, :] = placed * weight


def select(n, ids, route, tokens):
    count, width = tokens.shape
    out = pl.pallas_call(
        functools.partial(select_kernel, n),
        out_shape=[VMEM((n * SLAB, count), jnp.float32)]
        + [VMEM((SLAB, width), jnp.bfloat16)] * n,
        in_specs=[spec(VMEM)] * 3,
        out_specs=[spec(VMEM)] * (n + 1),
        compiler_params=pltpu.CompilerParams(vmem_limit_bytes=4 * MIB),
        name="select",
    )(ids, route, tokens)
    return out[0], out[1:]


def compact_kernel(n, *refs):
    slabs, rows_ref = refs[:n], refs[-1]
    full = jnp.concatenate([ref[...] for ref in slabs], axis=0)
    col = iota((n * SLOT, n * SLAB), 1)
    s = col % SLAB
    take = (iota((n * SLOT, n * SLAB), 0) == (col // SLAB) * SLOT + s) & (s < SLOT)
    rows_ref[...] = dot(take.astype(jnp.bfloat16), full).astype(jnp.bfloat16)


def compact(slabs, after):
    n, width = len(slabs), slabs[0].shape[1]
    return pl.pallas_call(
        functools.partial(compact_kernel, n),
        out_shape=VMEM((n * SLOT, width), jnp.bfloat16),
        in_specs=[spec(VMEM)] * (n + 1),
        out_specs=spec(VMEM),
        compiler_params=pltpu.CompilerParams(vmem_limit_bytes=4 * MIB),
        name="compact",
    )(*slabs, after)


def half_rows(unit, half, q):
    return pl.ds(pl.multiple_of((q ^ (unit // 2)) * 2 * half + (unit % 2) * half, 128), half)


def fetch_kernel(units, half, order_ref, gate_hbm, up_hbm, gate_ref, up_ref, sems):
    q = lax.axis_index("tensor")
    copies = []
    for i, unit in enumerate(units):
        at = half_rows(unit, half, q)
        copies.append(pltpu.make_async_copy(gate_hbm.at[at, :], gate_ref.at[i], sems.at[0, i]))
        copies.append(pltpu.make_async_copy(up_hbm.at[at, :], up_ref.at[i], sems.at[1, i]))
    for copy in copies:
        copy.start()
    for copy in copies:
        copy.wait()


def fetch(units, half, order, w_gate, w_up):
    shape = (len(units), half, w_gate.shape[1])
    return pl.pallas_call(
        functools.partial(fetch_kernel, units, half),
        out_shape=[VMEM(shape, jnp.bfloat16)] * 2,
        in_specs=[spec(VMEM)] + [spec(HBM)] * 2,
        out_specs=[spec(VMEM)] * 2,
        scratch_shapes=[pltpu.SemaphoreType.DMA((2, len(units)))],
        compiler_params=pltpu.CompilerParams(vmem_limit_bytes=2 * MIB),
        cost_estimate=pl.CostEstimate(
            flops=0, bytes_accessed=4 * shape[0] * shape[1] * shape[2], transcendentals=0
        ),
        name="fetch",
    )(order, w_gate, w_up)


def own_kernel(
    units, half, rows_ref, gate0, up0, gate_hbm, up_hbm, sum_g, sum_u, gate_ref, up_ref, sems
):
    q = lax.axis_index("tensor")
    copies = []
    for i, unit in enumerate(units):
        at = half_rows(unit, half, q)
        copies.append(pltpu.make_async_copy(gate_hbm.at[at, :], gate_ref.at[i], sems.at[0, i]))
        copies.append(pltpu.make_async_copy(up_hbm.at[at, :], up_ref.at[i], sems.at[1, i]))
    for copy in copies:
        copy.start()
    low, high = rows_ref[:, :half], rows_ref[:, half:]
    sum_g[...] = dot(low, gate0[0]) + dot(high, gate0[1])
    sum_u[...] = dot(low, up0[0]) + dot(high, up0[1])
    for copy in copies:
        copy.wait()


def own(units, half, rows, gate0, up0, w_gate, w_up):
    m, n = rows.shape[0], w_gate.shape[1]
    shape = (len(units), half, n)
    return pl.pallas_call(
        functools.partial(own_kernel, units, half),
        out_shape=[VMEM((m, n), jnp.float32)] * 2 + [VMEM(shape, jnp.bfloat16)] * 2,
        in_specs=[spec(VMEM)] * 3 + [spec(HBM)] * 2,
        out_specs=[spec(VMEM)] * 4,
        scratch_shapes=[pltpu.SemaphoreType.DMA((2, len(units)))],
        compiler_params=pltpu.CompilerParams(vmem_limit_bytes=4 * MIB),
        cost_estimate=pl.CostEstimate(
            flops=0, bytes_accessed=4 * shape[0] * shape[1] * shape[2], transcendentals=0
        ),
        name="own",
    )(rows, gate0, up0, w_gate, w_up)


def rest_kernel(parts, first, half, outs, *refs):
    rows = refs[: parts - 1]
    sum_g, sum_u, gate1, up1, gate_hbm, up_hbm, down_hbm = refs[parts - 1 : parts + 6]
    hidden_ref = refs[parts + 6]
    sent = refs[parts + 7 : parts + 7 + len(outs)]
    ring, down2, acc_g, acc_u, sems, down_sems = refs[parts + 7 + len(outs) :]
    q = lax.axis_index("tensor")
    count = 2 * parts
    queue = []
    for unit in range(first, count):
        for source in (gate_hbm, up_hbm):
            slot = len(queue) % (WINDOW + 1)
            at = half_rows(unit, half, q)
            queue.append(
                pltpu.make_async_copy(source.at[at, :], ring.at[slot], sems.at[slot])
            )
    jobs = len(queue)
    for i, k in enumerate(outs):
        at = pl.ds(pl.multiple_of((q ^ k) * 2 * half, 128), 2 * half)
        queue.append(pltpu.make_async_copy(down_hbm.at[:, at], down2.at[i], down_sems.at[i]))
    for copy in queue[:WINDOW]:
        copy.start()

    def arrive(job):
        queue[job].wait()
        if job + WINDOW < len(queue):
            queue[job + WINDOW].start()

    acc_g[...] = sum_g[...]
    acc_u[...] = sum_u[...]
    for unit in range(2, count):
        row = rows[unit // 2 - 1]
        row = row[:, half:] if unit % 2 else row[:, :half]
        if unit < first:
            acc_g[...] += dot(row, gate1[unit - 2])
            acc_u[...] += dot(row, up1[unit - 2])
        else:
            job = 2 * (unit - first)
            arrive(job)
            acc_g[...] += dot(row, ring[job % (WINDOW + 1)])
            arrive(job + 1)
            acc_u[...] += dot(row, ring[(job + 1) % (WINDOW + 1)])
    gate = acc_g[...]
    hidden = (gate / (1.0 + jnp.exp(-gate)) * acc_u[...]).astype(jnp.bfloat16)
    hidden_ref[...] = hidden
    for i in range(len(outs)):
        arrive(jobs + i)
        sent[i][...] = dot(hidden_ref[...], down2[i]).astype(jnp.bfloat16)


def rest(parts, first, half, outs, rows, sum_g, sum_u, gate1, up1, w_gate, w_up, w_down):
    m, n = sum_g.shape
    left = 2 * parts - first
    width = 2 * half
    return pl.pallas_call(
        functools.partial(rest_kernel, parts, first, half, outs),
        out_shape=[VMEM((m, n), jnp.bfloat16)] + [VMEM((m, width), jnp.bfloat16)] * len(outs),
        in_specs=[spec(VMEM)] * (parts - 1 + 4) + [spec(HBM)] * 3,
        out_specs=[spec(VMEM)] * (1 + len(outs)),
        scratch_shapes=[
            VMEM((WINDOW + 1, half, n), jnp.bfloat16),
            VMEM((len(outs), n, width), jnp.bfloat16),
            VMEM((m, n), jnp.float32),
            VMEM((m, n), jnp.float32),
            pltpu.SemaphoreType.DMA((WINDOW + 1,)),
            pltpu.SemaphoreType.DMA((len(outs),)),
        ],
        compiler_params=pltpu.CompilerParams(vmem_limit_bytes=30 * MIB),
        cost_estimate=pl.CostEstimate(
            flops=0, bytes_accessed=4 * left * half * n, transcendentals=0
        ),
        name="rest",
    )(*rows, sum_g, sum_u, gate1, up1, w_gate, w_up, w_down)


def down_kernel(outs, width, hidden_ref, down_hbm, *refs):
    sent = refs[: len(outs)]
    buf, sems = refs[len(outs) :]
    q = lax.axis_index("tensor")
    downs = []
    for i, k in enumerate(outs):
        at = pl.ds(pl.multiple_of((q ^ k) * width, 128), width)
        downs.append(pltpu.make_async_copy(down_hbm.at[:, at], buf.at[i], sems.at[i]))
    for copy in downs:
        copy.start()
    for i in range(len(outs)):
        downs[i].wait()
        sent[i][...] = dot(hidden_ref[...], buf[i]).astype(jnp.bfloat16)


def down(outs, width, hidden, w_down):
    m, n = hidden.shape
    return pl.pallas_call(
        functools.partial(down_kernel, outs, width),
        out_shape=[VMEM((m, width), jnp.bfloat16)] * len(outs),
        in_specs=[spec(VMEM), spec(HBM)],
        out_specs=[spec(VMEM)] * len(outs),
        scratch_shapes=[
            VMEM((len(outs), n, width), jnp.bfloat16),
            pltpu.SemaphoreType.DMA((len(outs),)),
        ],
        compiler_params=pltpu.CompilerParams(vmem_limit_bytes=20 * MIB),
        cost_estimate=pl.CostEstimate(
            flops=0, bytes_accessed=2 * len(outs) * n * width, transcendentals=0
        ),
        name="down",
    )(hidden, w_down)


def add_kernel(n, parts, *refs):
    terms, slabs = refs[:parts], refs[parts:]
    total = terms[0][...].astype(jnp.float32)
    for term in terms[1:]:
        total = total + term[...].astype(jnp.float32)
    total = total.astype(jnp.bfloat16)
    s, row = iota((SLAB, n * SLOT), 0), iota((SLAB, n * SLOT), 1)
    for k in range(n):
        take = (row == s + k * SLOT) & (s < SLOT)
        slabs[k][...] = dot(take.astype(jnp.bfloat16), total).astype(jnp.bfloat16)


def add(n, terms):
    width = terms[0].shape[1]
    return pl.pallas_call(
        functools.partial(add_kernel, n, len(terms)),
        out_shape=[VMEM((SLAB, width), jnp.bfloat16)] * n,
        in_specs=[spec(VMEM)] * len(terms),
        out_specs=[spec(VMEM)] * n,
        compiler_params=pltpu.CompilerParams(vmem_limit_bytes=4 * MIB),
        name="add",
    )(*terms)


def combine_kernel(n, comb_ref, *refs):
    slabs, out_ref = refs[:n], refs[n]
    full = jnp.concatenate([ref[...] for ref in slabs], axis=0)
    comb = comb_ref[...].T
    high = comb.astype(jnp.bfloat16)
    comb = comb - high.astype(jnp.float32)
    mid = comb.astype(jnp.bfloat16)
    low = (comb - mid.astype(jnp.float32)).astype(jnp.bfloat16)
    out_ref[...] = (dot(high, full) + (dot(mid, full) + dot(low, full))).astype(jnp.bfloat16)


def combine(comb, slabs):
    n, width = len(slabs), slabs[0].shape[1]
    return pl.pallas_call(
        functools.partial(combine_kernel, n),
        out_shape=jax.ShapeDtypeStruct((comb.shape[1], width), jnp.bfloat16),
        in_specs=[spec(VMEM)] * (n + 1),
        out_specs=spec(VMEM),
        compiler_params=pltpu.CompilerParams(vmem_limit_bytes=4 * MIB),
        name="combine",
    )(comb, *slabs)


def swap(x, axis, k):
    size = lax.axis_size(axis)
    return lax.ppermute(x, axis, [(i, i ^ k) for i in range(size)])


def per_device(tokens, expert_ids, route_weights, w_gate, w_up, w_down):
    n, parts = lax.axis_size("expert"), lax.axis_size("tensor")
    width = tokens.shape[1]
    half = width // 2
    w_gate, w_up, w_down = (
        pltpu.with_memory_space_constraint(w, HBM) for w in (w_gate, w_up, w_down)
    )
    comb, slabs = select(n, expert_ids.T, route_weights.T, tokens)
    slabs = [slabs[0]] + [swap(slabs[k], "expert", k) for k in range(1, n)]
    gate0, up0 = fetch(range(0, AHEAD0), half, comb, w_gate, w_up)
    mine = compact(slabs, gate0)
    rows = [swap(mine, "tensor", k) for k in range(1, parts)]
    first = AHEAD0 + AHEAD1
    sum_g, sum_u, gate1, up1 = own(range(AHEAD0, first), half, mine, gate0, up0, w_gate, w_up)
    early = list(range(parts - 1, 1, -1))
    hidden, *sent = rest(
        parts, first, half, early, rows, sum_g, sum_u, gate1, up1, w_gate, w_up, w_down
    )
    terms = [swap(x, "tensor", k) for k, x in zip(early, sent)]
    last, kept = down([1, 0], width, hidden, w_down)
    terms = [kept, swap(last, "tensor", 1)] + terms
    back = add(n, terms)
    back = [back[0]] + [swap(back[k], "expert", k) for k in range(1, n)]
    return combine(comb, back)


def solution(mesh):
    return jax.shard_map(
        per_device,
        mesh=mesh,
        in_specs=(
            P(("groups", "expert"), "tensor"),
            P(("groups", "expert"), None),
            P(("groups", "expert"), None),
            P(None, ("expert", "tensor")),
            P(None, ("expert", "tensor")),
            P(("expert", "tensor"), None),
        ),
        out_specs=P(("groups", "expert"), "tensor"),
        check_vma=False,
    )
```

```python
import functools

import jax
import jax.numpy as jnp
from jax import lax
from jax.experimental import pallas as pl
from jax.experimental.pallas import tpu as pltpu
from jax.sharding import PartitionSpec as P

E_W = 4
SLOT = 10
SLAB = 16
CUTS = (2, 5, 11)
RING = 3
DOWNS = 4
TILE = 512
MIB = 1 << 20
VMEM = pltpu.VMEM
HBM = pltpu.HBM
DMA = pltpu.SemaphoreType.DMA


def spec(space):
    return pl.BlockSpec(memory_space=space)


def limit(mib):
    return pltpu.CompilerParams(vmem_limit_bytes=mib * MIB)


def traffic(size):
    return pl.CostEstimate(flops=0, bytes_accessed=2 * size, transcendentals=0)


def dot(a, b):
    return lax.dot_general(a, b, (((1,), (0,)), ((), ())), preferred_element_type=jnp.float32)


def iota(shape, dim):
    return lax.broadcasted_iota(jnp.int32, shape, dim)


def job_copy(job, half, gate_hbm, up_hbm, target, sem):
    q = lax.axis_index("tensor")
    unit = job // 2
    start = (q ^ (unit // 2)) * 2 * half + (unit % 2) * half
    at = pl.ds(pl.multiple_of(start, 128), half)
    return pltpu.make_async_copy((up_hbm if job % 2 else gate_hbm).at[at, :], target, sem)


def job_copies(jobs, half, gate_hbm, up_hbm, targets, sems):
    return [
        job_copy(job, half, gate_hbm, up_hbm, targets[i], sems.at[i])
        for i, job in enumerate(jobs)
    ]


def half_of(rows, job):
    half = rows.shape[1] // 2
    return rows[:, half:] if job // 2 % 2 else rows[:, :half]


def select_kernel(n, jobs, half, ids_hbm, route_hbm, tok_hbm, gate_hbm, up_hbm, *refs):
    comb_ref, slabs, held = refs[0], refs[1 : n + 1], refs[n + 1 : -5]
    ids_ref, route_ref, tok_ref, sems, held_sems = refs[-5:]
    inputs = [
        pltpu.make_async_copy(source, target, sems.at[i])
        for i, (source, target) in enumerate(
            ((ids_hbm, ids_ref), (route_hbm, route_ref), (tok_hbm, tok_ref))
        )
    ]
    copies = job_copies(jobs, half, gate_hbm, up_hbm, held, held_sems)
    for copy in inputs + copies:
        copy.start()
    for copy in inputs:
        copy.wait()
    me = lax.axis_index("expert")
    replicas = n // E_W
    ids, route, tok = ids_ref[...], route_ref[...], tok_ref[...]
    count = tok.shape[0]
    before = (iota((count, count), 0) <= iota((count, count), 1)).astype(jnp.bfloat16)
    slot = iota((SLAB, count), 0).astype(jnp.float32)
    for k in range(n):
        hit = ids == (me ^ k) // replicas
        member = jnp.sum(jnp.where(hit, 1.0, 0.0), axis=0, keepdims=True)
        weight = jnp.sum(jnp.where(hit, route, 0.0), axis=0, keepdims=True)
        member = jnp.broadcast_to(member, (SLAB, count))
        position = dot(member.astype(jnp.bfloat16), before) - 1.0
        placed = jnp.where(position == slot, member, 0.0)
        slabs[k][...] = dot(placed.astype(jnp.bfloat16), tok).astype(jnp.bfloat16)
        comb_ref[k * SLAB : (k + 1) * SLAB, :] = placed * weight
    for copy in copies:
        copy.wait()


def select(n, jobs, ids, route, tokens, w_gate, w_up):
    count, width = tokens.shape
    held = VMEM((width // 2, w_gate.shape[1]), jnp.bfloat16)
    out = pl.pallas_call(
        functools.partial(select_kernel, n, jobs, width // 2),
        out_shape=[VMEM((n * SLAB, count), jnp.float32)]
        + [VMEM((SLAB, width), jnp.bfloat16)] * n
        + [held] * len(jobs),
        in_specs=[spec(HBM)] * 5,
        out_specs=[spec(VMEM)] * (n + 1 + len(jobs)),
        scratch_shapes=[
            VMEM(ids.shape, ids.dtype),
            VMEM(route.shape, route.dtype),
            VMEM(tokens.shape, tokens.dtype),
            DMA((3,)),
            DMA((len(jobs),)),
        ],
        compiler_params=limit(4),
        name="select",
    )(ids, route, tokens, w_gate, w_up)
    return out[0], out[1 : n + 1], out[n + 1 :]


def compact_kernel(n, *refs):
    slabs, rows_ref = refs[:n], refs[-1]
    full = jnp.concatenate([ref[...] for ref in slabs], axis=0)
    col = iota((n * SLOT, n * SLAB), 1)
    s = col % SLAB
    take = (iota((n * SLOT, n * SLAB), 0) == (col // SLAB) * SLOT + s) & (s < SLOT)
    rows_ref[...] = dot(take.astype(jnp.bfloat16), full).astype(jnp.bfloat16)


def compact(slabs, after):
    n, width = len(slabs), slabs[0].shape[1]
    return pl.pallas_call(
        functools.partial(compact_kernel, n),
        out_shape=VMEM((n * SLOT, width), jnp.bfloat16),
        in_specs=[spec(VMEM)] * (n + 1),
        out_specs=spec(VMEM),
        compiler_params=limit(4),
        name="compact",
    )(*slabs, after)


def fetch_kernel(jobs, half, order_ref, gate_hbm, up_hbm, *refs):
    held, sems = refs[:-1], refs[-1]
    copies = job_copies(jobs, half, gate_hbm, up_hbm, held, sems)
    for copy in copies:
        copy.start()
    for copy in copies:
        copy.wait()


def fetch(jobs, half, order, w_gate, w_up):
    shape = (half, w_gate.shape[1])
    return pl.pallas_call(
        functools.partial(fetch_kernel, jobs, half),
        out_shape=[VMEM(shape, jnp.bfloat16)] * len(jobs),
        in_specs=[spec(VMEM)] + [spec(HBM)] * 2,
        out_specs=[spec(VMEM)] * len(jobs),
        scratch_shapes=[DMA((len(jobs),))],
        compiler_params=limit(2),
        cost_estimate=traffic(len(jobs) * shape[0] * shape[1]),
        name="fetch",
    )(order, w_gate, w_up)


def own_kernel(jobs, half, rows_ref, *refs):
    weights, gate_hbm, up_hbm, sum_g, sum_u = refs[:4], *refs[4:8]
    held, sems = refs[8:-1], refs[-1]
    copies = job_copies(jobs, half, gate_hbm, up_hbm, held, sems)
    for copy in copies:
        copy.start()
    n = gate_hbm.shape[1]
    tile = min(TILE, n)
    low, high = rows_ref[:, :half], rows_ref[:, half:]
    steps = [(out, job, at) for job, out in ((0, sum_g), (1, sum_u)) for at in range(0, n, tile)]
    done = 0
    for i, (out, job, at) in enumerate(steps):
        at = slice(at, at + tile)
        out[:, at] = dot(low, weights[job][:, at]) + dot(high, weights[job + 2][:, at])
        while done < len(copies) and done * len(steps) < (i + 1) * len(copies):
            copies[done].wait()
            done += 1
    for copy in copies[done:]:
        copy.wait()


def own(jobs, half, rows, held, w_gate, w_up):
    m, n = rows.shape[0], w_gate.shape[1]
    shape = (half, n)
    return pl.pallas_call(
        functools.partial(own_kernel, jobs, half),
        out_shape=[VMEM((m, n), jnp.float32)] * 2 + [VMEM(shape, jnp.bfloat16)] * len(jobs),
        in_specs=[spec(VMEM)] * 5 + [spec(HBM)] * 2,
        out_specs=[spec(VMEM)] * (2 + len(jobs)),
        scratch_shapes=[DMA((len(jobs),))],
        compiler_params=limit(4),
        cost_estimate=traffic(len(jobs) * shape[0] * shape[1]),
        name="own",
    )(rows, *held, w_gate, w_up)


def down_copy(k, down_hbm, target, sem):
    width = target.shape[1]
    q = lax.axis_index("tensor")
    at = pl.ds(pl.multiple_of((q ^ k) * width, 128), width)
    return pltpu.make_async_copy(down_hbm.at[:, at], target, sem)


def rest_kernel(parts, first, half, outs, *refs):
    rows, refs = refs[: parts - 1], refs[parts - 1 :]
    held, refs = refs[: first - 4], refs[first - 4 :]
    sum_g, sum_u, gate_hbm, up_hbm, down_hbm = refs[:5]
    hidden_ref, sent = refs[5], refs[6 : 6 + len(outs)]
    ring, down2, acc_g, acc_u, sems, down_sems = refs[6 + len(outs) :]
    count = 4 * parts
    slots, deep = down2.shape[:2]
    cuts = hidden_ref.shape[1] // deep

    weights = []
    for i, job in enumerate(range(first, count)):
        slot = i % ring.shape[0]
        weights.append(job_copy(job, half, gate_hbm, up_hbm, ring.at[slot], sems.at[slot]))
    downs = []
    for i in range(cuts * len(outs)):
        rows_at, slot = down_hbm.at[pl.ds(i % cuts * deep, deep), :], i % slots
        downs.append(down_copy(outs[i // cuts], rows_at, down2.at[slot], down_sems.at[slot]))
    for copy in weights[: ring.shape[0]] + downs[:1]:
        copy.start()
    ahead = 1

    def more_downs(number):
        nonlocal ahead
        for copy in downs[ahead : min(ahead + number, slots)]:
            copy.start()
            ahead += 1

    def add(job, weight):
        row = half_of(rows[job // 4 - 1], job)
        acc = acc_u if job % 2 else acc_g
        acc[...] += dot(row, weight[...])

    acc_g[...] = sum_g[...]
    acc_u[...] = sum_u[...]
    now = 4
    for i, job in enumerate(range(first, count)):
        until = 4 + (first - 4) * (i + 1) // len(weights)
        for held_job in range(now, until):
            add(held_job, held[held_job - 4])
        now = until
        weights[i].wait()
        add(job, ring.at[i % ring.shape[0]])
        if i + ring.shape[0] < len(weights):
            weights[i + ring.shape[0]].start()
        else:
            more_downs(1)
    more_downs(slots)
    gate = acc_g[...]
    hidden_ref[...] = (gate / (1.0 + jnp.exp(-gate)) * acc_u[...]).astype(jnp.bfloat16)
    for i in range(len(outs)):
        total = None
        for j in range(cuts):
            at = cuts * i + j
            downs[at].wait()
            part = dot(hidden_ref[:, j * deep : (j + 1) * deep], down2[at % slots])
            total = part if total is None else total + part
            if at + slots < len(downs):
                downs[at + slots].start()
        sent[i][...] = total.astype(jnp.bfloat16)


def rest(parts, half, outs, rows, held, sum_g, sum_u, w_gate, w_up, w_down):
    m, n = sum_g.shape
    width = 2 * half
    first = 4 + len(held)
    size = ((4 * parts - first) * half + len(outs) * width) * n
    cuts = 2 if n % 256 == 0 else 1
    return pl.pallas_call(
        functools.partial(rest_kernel, parts, first, half, outs),
        out_shape=[VMEM((m, n), jnp.bfloat16)]
        + [VMEM((m, width), jnp.bfloat16)] * len(outs),
        in_specs=[spec(VMEM)] * (parts + 1 + len(held)) + [spec(HBM)] * 3,
        out_specs=[spec(VMEM)] * (1 + len(outs)),
        scratch_shapes=[
            VMEM((RING, half, n), jnp.bfloat16),
            VMEM((DOWNS, n // cuts, width), jnp.bfloat16),
            VMEM((m, n), jnp.float32),
            VMEM((m, n), jnp.float32),
            DMA((RING,)),
            DMA((DOWNS,)),
        ],
        compiler_params=limit(26),
        cost_estimate=traffic(size),
        name="rest",
    )(*rows, *held, sum_g, sum_u, w_gate, w_up, w_down)


def near_kernel(hidden_ref, down_hbm, sent, next_ref, buf, sems):
    cuts, deep = buf.shape[:2]
    copies = []
    for j in range(cuts):
        rows_at = down_hbm.at[pl.ds(j * deep, deep), :]
        copies.append(down_copy(1, rows_at, buf.at[j], sems.at[j]))
    for j in range(cuts):
        at = pl.ds(j * deep, deep)
        copies.append(down_copy(0, down_hbm.at[at, :], next_ref.at[at, :], sems.at[cuts + j]))
    for copy in copies:
        copy.start()
    total = None
    for j in range(cuts):
        copies[j].wait()
        part = dot(hidden_ref[:, j * deep : (j + 1) * deep], buf[j])
        total = part if total is None else total + part
    sent[...] = total.astype(jnp.bfloat16)
    for copy in copies[cuts:]:
        copy.wait()


def near(width, hidden, w_down):
    m, n = hidden.shape
    cuts = 2 if n % 256 == 0 else 1
    return pl.pallas_call(
        near_kernel,
        out_shape=[VMEM((m, width), jnp.bfloat16), VMEM((n, width), jnp.bfloat16)],
        in_specs=[spec(VMEM), spec(HBM)],
        out_specs=[spec(VMEM)] * 2,
        scratch_shapes=[VMEM((cuts, n // cuts, width), jnp.bfloat16), DMA((2 * cuts,))],
        compiler_params=limit(12),
        cost_estimate=traffic(2 * n * width),
        name="near",
    )(hidden, w_down)


def keep_kernel(hidden_ref, weight_ref, *refs):
    terms, total_ref = refs[:-1], refs[-1]
    total = dot(hidden_ref[...], weight_ref[...])
    for term in terms:
        total = total + term[...].astype(jnp.float32)
    total_ref[...] = total


def keep(hidden, weight, terms):
    m, width = hidden.shape[0], weight.shape[1]
    return pl.pallas_call(
        keep_kernel,
        out_shape=VMEM((m, width), jnp.float32),
        in_specs=[spec(VMEM)] * (2 + len(terms)),
        out_specs=spec(VMEM),
        compiler_params=limit(4),
        cost_estimate=traffic(weight.size // 2),
        name="keep",
    )(hidden, weight, *terms)


def add_kernel(n, total_ref, term_ref, *slabs):
    total = (total_ref[...] + term_ref[...].astype(jnp.float32)).astype(jnp.bfloat16)
    s, row = iota((SLAB, n * SLOT), 0), iota((SLAB, n * SLOT), 1)
    for k in range(n):
        take = (row == s + k * SLOT) & (s < SLOT)
        slabs[k][...] = dot(take.astype(jnp.bfloat16), total).astype(jnp.bfloat16)


def add(n, total, term):
    return pl.pallas_call(
        functools.partial(add_kernel, n),
        out_shape=[VMEM((SLAB, total.shape[1]), jnp.bfloat16)] * n,
        in_specs=[spec(VMEM)] * 2,
        out_specs=[spec(VMEM)] * n,
        compiler_params=limit(4),
        name="add",
    )(total, term)


def combine_kernel(n, comb_ref, *refs):
    slabs, out_ref = refs[:n], refs[n]
    full = jnp.concatenate([ref[...] for ref in slabs], axis=0)
    comb = comb_ref[...].T
    high = comb.astype(jnp.bfloat16)
    comb = comb - high.astype(jnp.float32)
    mid = comb.astype(jnp.bfloat16)
    low = (comb - mid.astype(jnp.float32)).astype(jnp.bfloat16)
    out_ref[...] = (dot(high, full) + (dot(mid, full) + dot(low, full))).astype(jnp.bfloat16)


def combine(comb, slabs):
    n, width = len(slabs), slabs[0].shape[1]
    return pl.pallas_call(
        functools.partial(combine_kernel, n),
        out_shape=jax.ShapeDtypeStruct((comb.shape[1], width), jnp.bfloat16),
        in_specs=[spec(VMEM)] * (n + 1),
        out_specs=spec(VMEM),
        compiler_params=limit(4),
        name="combine",
    )(comb, *slabs)


def swap(x, axis, k):
    size = lax.axis_size(axis)
    return lax.ppermute(x, axis, [(i, i ^ k) for i in range(size)])


def per_device(*args):
    tokens, ids, route, w_gate, w_up, w_down = (
        pltpu.with_memory_space_constraint(x, HBM)
        for x in (args[0], args[1].T, args[2].T, *args[3:])
    )
    n, parts = lax.axis_size("expert"), lax.axis_size("tensor")
    half = tokens.shape[1] // 2
    comb, slabs, held = select(n, range(CUTS[0]), ids, route, tokens, w_gate, w_up)
    slabs = [slabs[0]] + [swap(slabs[k], "expert", k) for k in range(1, n)]
    held += fetch(range(CUTS[0], CUTS[1]), half, comb, w_gate, w_up)
    mine = compact(slabs, held[-1])
    rows = [swap(mine, "tensor", k) for k in range(1, parts)]
    sum_g, sum_u, *more = own(range(CUTS[1], CUTS[2]), half, mine, held[:4], w_gate, w_up)
    held = [*held[4:], *more]
    far = list(range(parts - 1, 1, -1))
    hidden, *sent = rest(
        parts, half, far, rows, held, sum_g, sum_u, w_gate, w_up, w_down
    )
    terms = [swap(x, "tensor", k) for k, x in zip(far, sent)]
    sent, weight0 = near(2 * half, hidden, w_down)
    last = swap(sent, "tensor", 1)
    total = keep(hidden, weight0, terms)
    back = add(n, total, last)
    back = [back[0]] + [swap(back[k], "expert", k) for k in range(1, n)]
    return combine(comb, back)


def solution(mesh):
    return jax.shard_map(
        per_device,
        mesh=mesh,
        in_specs=(
            P(("groups", "expert"), "tensor"),
            P(("groups", "expert"), None),
            P(("groups", "expert"), None),
            P(None, ("expert", "tensor")),
            P(None, ("expert", "tensor")),
            P(("expert", "tensor"), None),
        ),
        out_specs=P(("groups", "expert"), "tensor"),
        check_vma=False,
    )
```

```python
import functools

import jax
import jax.numpy as jnp
from jax import lax
from jax.experimental import pallas as pl
from jax.experimental.pallas import tpu as pltpu
from jax.sharding import PartitionSpec as P

E_W = 4
SLOT = 10
SLAB = 16
FETCH = 2
OWN = 5
DOWNS = 3
TILE = 512
WIDE = 512
MICRO = 1_150_000_000
MIB = 1 << 20
VMEM = pltpu.VMEM
HBM = pltpu.HBM
DMA = pltpu.SemaphoreType.DMA


def spec(space):
    return pl.BlockSpec(memory_space=space)


def limit(mib):
    return pltpu.CompilerParams(vmem_limit_bytes=mib * MIB)


def lasts(micros):
    return pl.CostEstimate(flops=int(micros * MICRO), bytes_accessed=0, transcendentals=0)


def dot(a, b):
    return lax.dot_general(a, b, (((1,), (0,)), ((), ())), preferred_element_type=jnp.float32)


def iota(shape, dim):
    return lax.broadcasted_iota(jnp.int32, shape, dim)


def job_copies(jobs, half, up_hbm, targets, sems):
    q = lax.axis_index("tensor")
    copies = []
    for i, job in enumerate(jobs):
        start = (q ^ (job // 2)) * 2 * half + (job % 2) * half
        at = pl.ds(pl.multiple_of(start, 128), half)
        copies.append(pltpu.make_async_copy(up_hbm.at[at, :], targets[i], sems.at[i]))
    return copies


def select_kernel(n, ids_hbm, route_hbm, tok_hbm, comb_ref, *refs):
    slabs, (ids_ref, route_ref, tok_ref, sems) = refs[:n], refs[n:]
    inputs = [
        pltpu.make_async_copy(source, target, sems.at[i])
        for i, (source, target) in enumerate(
            ((ids_hbm, ids_ref), (route_hbm, route_ref), (tok_hbm, tok_ref))
        )
    ]
    for copy in inputs:
        copy.start()
    for copy in inputs:
        copy.wait()
    me = lax.axis_index("expert")
    replicas = n // E_W
    ids, route, tok = ids_ref[...], route_ref[...], tok_ref[...]
    count = tok.shape[0]
    before = (iota((count, count), 0) <= iota((count, count), 1)).astype(jnp.bfloat16)
    slot = iota((SLAB, count), 0).astype(jnp.float32)
    for k in range(n):
        hit = ids == (me ^ k) // replicas
        member = jnp.sum(jnp.where(hit, 1.0, 0.0), axis=0, keepdims=True)
        weight = jnp.sum(jnp.where(hit, route, 0.0), axis=0, keepdims=True)
        member = jnp.broadcast_to(member, (SLAB, count))
        position = dot(member.astype(jnp.bfloat16), before) - 1.0
        placed = jnp.where(position == slot, member, 0.0)
        slabs[k][...] = dot(placed.astype(jnp.bfloat16), tok).astype(jnp.bfloat16)
        comb_ref[k * SLAB : (k + 1) * SLAB, :] = placed * weight


def select(n, ids, route, tokens):
    count, width = tokens.shape
    out = pl.pallas_call(
        functools.partial(select_kernel, n),
        out_shape=[VMEM((n * SLAB, count), jnp.float32)]
        + [VMEM((SLAB, width), jnp.bfloat16)] * n,
        in_specs=[spec(HBM)] * 3,
        out_specs=[spec(VMEM)] * (n + 1),
        scratch_shapes=[
            VMEM(ids.shape, ids.dtype),
            VMEM(route.shape, route.dtype),
            VMEM(tokens.shape, tokens.dtype),
            DMA((3,)),
        ],
        compiler_params=limit(4),
        cost_estimate=lasts(40),
        name="select",
    )(ids, route, tokens)
    return out[0], out[1:]


def compact_kernel(n, *refs):
    slabs, rows_ref = refs[:n], refs[-1]
    full = jnp.concatenate([ref[...] for ref in slabs], axis=0)
    col = iota((n * SLOT, n * SLAB), 1)
    s = col % SLAB
    take = (iota((n * SLOT, n * SLAB), 0) == (col // SLAB) * SLOT + s) & (s < SLOT)
    rows_ref[...] = dot(take.astype(jnp.bfloat16), full).astype(jnp.bfloat16)


def compact(slabs, after):
    n, width = len(slabs), slabs[0].shape[1]
    return pl.pallas_call(
        functools.partial(compact_kernel, n),
        out_shape=VMEM((n * SLOT, width), jnp.bfloat16),
        in_specs=[spec(VMEM)] * (n + 1),
        out_specs=spec(VMEM),
        compiler_params=limit(4),
        name="compact",
    )(*slabs, after)


def chunk(weight_ref, k, width, side, half, tile):
    start = (lax.axis_index("tensor") ^ k) * width + side
    return weight_ref[pl.ds(pl.multiple_of(start, 128), half), tile]


def tiles(n):
    return [slice(at, at + min(TILE, n)) for at in range(0, n, min(TILE, n))]


def fetch_kernel(jobs, half, order_ref, up_hbm, *refs):
    held, sems = refs[:-1], refs[-1]
    copies = job_copies(jobs, half, up_hbm, held, sems)
    for copy in copies:
        copy.start()
    for copy in copies:
        copy.wait()


def fetch(jobs, half, order, w_up):
    shape = (half, w_up.shape[1])
    return pl.pallas_call(
        functools.partial(fetch_kernel, jobs, half),
        out_shape=[VMEM(shape, jnp.bfloat16)] * len(jobs),
        in_specs=[spec(VMEM), spec(HBM)],
        out_specs=[spec(VMEM)] * len(jobs),
        scratch_shapes=[DMA((len(jobs),))],
        compiler_params=limit(2),
        cost_estimate=lasts(0.2),
        name="fetch",
    )(order, w_up)


def own_kernel(jobs, rows_ref, up_low, up_high, up_hbm, sum_u, *refs):
    held, sems = refs[:-1], refs[-1]
    half = rows_ref.shape[1] // 2
    copies = job_copies(jobs, half, up_hbm, held, sems)
    for copy in copies:
        copy.start()
    low, high = rows_ref[:, :half], rows_ref[:, half:]
    steps = tiles(sum_u.shape[1])
    done = 0
    for i, tile in enumerate(steps):
        sum_u[:, tile] = dot(low, up_low[:, tile]) + dot(high, up_high[:, tile])
        while done < len(copies) and done * len(steps) < (i + 1) * len(copies):
            copies[done].wait()
            done += 1
    for copy in copies[done:]:
        copy.wait()


def own(jobs, rows, held, w_up):
    (m, width), n = rows.shape, w_up.shape[1]
    return pl.pallas_call(
        functools.partial(own_kernel, jobs),
        out_shape=[VMEM((m, n), jnp.float32)]
        + [VMEM((width // 2, n), jnp.bfloat16)] * len(jobs),
        in_specs=[spec(VMEM)] * 3 + [spec(HBM)],
        out_specs=[spec(VMEM)] * (1 + len(jobs)),
        scratch_shapes=[DMA((len(jobs),))],
        compiler_params=limit(2),
        cost_estimate=lasts(0.2),
        name="own",
    )(rows, *held, w_up)


def down_copy(k, down_hbm, target, sem):
    width = target.shape[1]
    q = lax.axis_index("tensor")
    at = pl.ds(pl.multiple_of((q ^ k) * width, 128), width)
    return pltpu.make_async_copy(down_hbm.at[:, at], target, sem)


def rest_kernel(outs, first, *refs):
    parts = len(outs) + 2
    rows, refs = refs[:parts], refs[parts:]
    held, refs = refs[: first - 2], refs[first - 2 :]
    start_u, gate_ref, up_hbm, down_hbm, hidden_ref = refs[:5]
    sent, refs = refs[5 : 5 + len(outs)], refs[5 + len(outs) :]
    late, down2, sum_g, late_sems, down_sems = refs
    width = rows[0].shape[1]
    half = width // 2
    slots, deep = down2.shape[:2]
    n = hidden_ref.shape[1]
    wide = min(WIDE, n)
    deep_gate = 256 if width % 256 == 0 else 128
    cuts = n // deep
    jobs = range(first, 2 * parts)
    lates = job_copies(jobs, half, up_hbm, [late.at[i] for i in range(len(jobs))], late_sems)
    downs = []
    for i in range(cuts * len(outs)):
        rows_at, slot = down_hbm.at[pl.ds(i % cuts * deep, deep), :], i % slots
        downs.append(down_copy(outs[i // cuts], rows_at, down2.at[slot], down_sems.at[slot]))
    for copy in lates:
        copy.start()
    ups = list(held) + [late.at[i] for i in range(len(jobs))]

    def gate_part(step):
        at = pl.ds(pl.multiple_of(step * wide, 128), wide)
        total = None
        for k in range(parts):
            for side in range(0, width, deep_gate):
                row = rows[k][:, side : side + deep_gate]
                part = dot(row, chunk(gate_ref, k, width, side, deep_gate, at))
                total = part if total is None else total + part
        sum_g[:, at] = total

    middle = n // wide // 2
    pl.loop(0, middle)(gate_part)
    for copy in downs[:slots]:
        copy.start()
    pl.loop(middle, n // wide)(gate_part)
    for copy in lates:
        copy.wait()

    @pl.loop(0, n // wide)
    def _(step):
        at = pl.ds(pl.multiple_of(step * wide, 128), wide)
        total = start_u[:, at]
        for k in range(1, parts):
            total += dot(rows[k][:, :half], ups[2 * k - 2][:, at])
            total += dot(rows[k][:, half:], ups[2 * k - 1][:, at])
        gate = sum_g[:, at]
        hidden_ref[:, at] = (gate / (1.0 + jnp.exp(-gate)) * total).astype(jnp.bfloat16)

    for i in range(len(outs)):
        for j in range(cuts):
            piece = cuts * i + j
            downs[piece].wait()

            @pl.loop(0, 2)
            def _(step):
                at = pl.ds(pl.multiple_of(step * half, 128), half)
                mid = hidden_ref[:, j * deep : (j + 1) * deep]
                part = dot(mid, down2[piece % slots, :, at])
                if j > 0:
                    part += sum_g[:, at]
                if j < cuts - 1:
                    sum_g[:, at] = part
                else:
                    sent[i][:, at] = part.astype(jnp.bfloat16)

            if piece + slots < len(downs):
                downs[piece + slots].start()


def rest(outs, rows, held, sum_u, w_gate, w_up, w_down):
    m, n = sum_u.shape
    width = rows[0].shape[1]
    cuts = 2 if n % 256 == 0 else 1
    first = 2 + len(held)
    late = max(1, 2 * len(rows) - first)
    return pl.pallas_call(
        functools.partial(rest_kernel, outs, first),
        out_shape=[VMEM((m, n), jnp.bfloat16)] + [VMEM((m, width), jnp.bfloat16)] * len(outs),
        in_specs=[spec(VMEM)] * (len(rows) + len(held) + 2) + [spec(HBM)] * 2,
        out_specs=[spec(VMEM)] * (1 + len(outs)),
        scratch_shapes=[
            VMEM((late, width // 2, n), jnp.bfloat16),
            VMEM((DOWNS, n // cuts, width), jnp.bfloat16),
            VMEM((m, max(n, width)), jnp.float32),
            DMA((late,)),
            DMA((DOWNS,)),
        ],
        compiler_params=limit(19),
        cost_estimate=lasts(10),
        name="rest",
    )(*rows, *held, sum_u, w_gate, w_up, w_down)


def near_kernel(hidden_ref, down_hbm, sent, next_ref, buf, total, sems):
    cuts, deep = buf.shape[:2]
    copies = []
    for j in range(cuts):
        rows_at = down_hbm.at[pl.ds(j * deep, deep), :]
        copies.append(down_copy(1, rows_at, buf.at[j], sems.at[j]))
    for j in range(cuts):
        at = pl.ds(j * deep, deep)
        copies.append(down_copy(0, down_hbm.at[at, :], next_ref.at[at, :], sems.at[cuts + j]))
    for copy in copies:
        copy.start()
    for j in range(cuts):
        copies[j].wait()
        mid = hidden_ref[:, j * deep : (j + 1) * deep]
        for tile in tiles(sent.shape[1]):
            part = dot(mid, buf[j, :, tile])
            if j > 0:
                part += total[:, tile]
            if j < cuts - 1:
                total[:, tile] = part
            else:
                sent[:, tile] = part.astype(jnp.bfloat16)
    for copy in copies[cuts:]:
        copy.wait()


def near(width, hidden, w_down):
    m, n = hidden.shape
    cuts = 2 if n % 256 == 0 else 1
    return pl.pallas_call(
        near_kernel,
        out_shape=[VMEM((m, width), jnp.bfloat16), VMEM((n, width), jnp.bfloat16)],
        in_specs=[spec(VMEM), spec(HBM)],
        out_specs=[spec(VMEM)] * 2,
        scratch_shapes=[
            VMEM((cuts, n // cuts, width), jnp.bfloat16),
            VMEM((m, width), jnp.float32),
            DMA((2 * cuts,)),
        ],
        compiler_params=limit(12),
        cost_estimate=lasts(4),
        name="near",
    )(hidden, w_down)


def keep_kernel(hidden_ref, weight_ref, total_ref):
    total_ref[...] = dot(hidden_ref[...], weight_ref[...])


def keep(hidden, weight):
    m, width = hidden.shape[0], weight.shape[1]
    return pl.pallas_call(
        keep_kernel,
        out_shape=VMEM((m, width), jnp.float32),
        in_specs=[spec(VMEM)] * 2,
        out_specs=spec(VMEM),
        compiler_params=limit(4),
        cost_estimate=lasts(1),
        name="keep",
    )(hidden, weight)


def gather_kernel(total_ref, *refs):
    terms, sum_ref = refs[:-1], refs[-1]
    total = total_ref[...]
    for term in terms:
        total = total + term[...].astype(jnp.float32)
    sum_ref[...] = total


def gather(total, terms):
    return pl.pallas_call(
        gather_kernel,
        out_shape=VMEM(total.shape, jnp.float32),
        in_specs=[spec(VMEM)] * (1 + len(terms)),
        out_specs=spec(VMEM),
        compiler_params=limit(4),
        cost_estimate=lasts(2),
        name="gather",
    )(total, *terms)


def add_kernel(n, total_ref, *refs):
    terms, slabs = refs[:-n], refs[-n:]
    total = total_ref[...]
    for term in terms:
        total = total + term[...].astype(jnp.float32)
    total = total.astype(jnp.bfloat16)
    s, row = iota((SLAB, n * SLOT), 0), iota((SLAB, n * SLOT), 1)
    for k in range(n):
        take = (row == s + k * SLOT) & (s < SLOT)
        slabs[k][...] = dot(take.astype(jnp.bfloat16), total).astype(jnp.bfloat16)


def add(n, total, terms):
    return pl.pallas_call(
        functools.partial(add_kernel, n),
        out_shape=[VMEM((SLAB, total.shape[1]), jnp.bfloat16)] * n,
        in_specs=[spec(VMEM)] * (1 + len(terms)),
        out_specs=[spec(VMEM)] * n,
        compiler_params=limit(4),
        name="add",
    )(total, *terms)


def combine_kernel(n, comb_ref, *refs):
    slabs, out_ref = refs[:n], refs[n]
    full = jnp.concatenate([ref[...] for ref in slabs], axis=0)
    comb = comb_ref[...].T
    high = comb.astype(jnp.bfloat16)
    comb = comb - high.astype(jnp.float32)
    mid = comb.astype(jnp.bfloat16)
    low = (comb - mid.astype(jnp.float32)).astype(jnp.bfloat16)
    out_ref[...] = (dot(high, full) + (dot(mid, full) + dot(low, full))).astype(jnp.bfloat16)


def combine(comb, slabs):
    n, width = len(slabs), slabs[0].shape[1]
    return pl.pallas_call(
        functools.partial(combine_kernel, n),
        out_shape=jax.ShapeDtypeStruct((comb.shape[1], width), jnp.bfloat16),
        in_specs=[spec(VMEM)] * (n + 1),
        out_specs=spec(VMEM),
        compiler_params=limit(4),
        name="combine",
    )(comb, *slabs)


def swap(x, axis, k):
    size = lax.axis_size(axis)
    return lax.ppermute(x, axis, [(i, i ^ k) for i in range(size)])


def per_device(*args):
    tokens, ids, route, w_up, w_down = (
        pltpu.with_memory_space_constraint(x, HBM)
        for x in (args[0], args[1].T, args[2].T, args[4], args[5])
    )
    w_gate = args[3]
    n, parts = lax.axis_size("expert"), lax.axis_size("tensor")
    width = tokens.shape[1]
    comb, slabs = select(n, ids, route, tokens)
    slabs = [slabs[0]] + [swap(slabs[k], "expert", k) for k in range(1, n)]
    held = fetch(range(FETCH), width // 2, comb, w_up)
    mine = compact(slabs, held[-1])
    rows = [mine] + [swap(mine, "tensor", k) for k in range(1, parts)]
    sum_u, *more = own(range(FETCH, OWN), mine, held[:2], w_up)
    held = [*held[2:], *more]
    far = list(range(parts - 1, 1, -1))
    hidden, *sent = rest(far, rows, held, sum_u, w_gate, w_up, w_down)
    terms = [swap(x, "tensor", k) for k, x in zip(far, sent)]
    sent, weight0 = near(width, hidden, w_down)
    last = swap(sent, "tensor", 1)
    total = gather(keep(hidden, weight0), terms)
    back = add(n, total, [last])
    back = [back[0]] + [swap(back[k], "expert", k) for k in range(1, n)]
    return combine(comb, back)


def solution(mesh):
    return jax.shard_map(
        per_device,
        mesh=mesh,
        in_specs=(
            P(("groups", "expert"), "tensor"),
            P(("groups", "expert"), None),
            P(("groups", "expert"), None),
            P(None, ("expert", "tensor")),
            P(None, ("expert", "tensor")),
            P(("expert", "tensor"), None),
        ),
        out_specs=P(("groups", "expert"), "tensor"),
        check_vma=False,
    )
```

```python
import functools

import jax
import jax.numpy as jnp
from jax import lax
from jax.experimental import pallas as pl
from jax.experimental.pallas import tpu as pltpu
from jax.sharding import PartitionSpec as P

E_W = 4
SLOT = 10
SLAB = 16
FETCH = 2
OWN = 4
DOWNS = 3
TILE = 512
WIDE = 512
MICRO = 1_150_000_000
MIB = 1 << 20
VMEM = pltpu.VMEM
HBM = pltpu.HBM
DMA = pltpu.SemaphoreType.DMA


def spec(space):
    return pl.BlockSpec(memory_space=space)


def limit(mib):
    return pltpu.CompilerParams(vmem_limit_bytes=mib * MIB)


def lasts(micros):
    return pl.CostEstimate(flops=int(micros * MICRO), bytes_accessed=0, transcendentals=0)


def dot(a, b):
    return lax.dot_general(a, b, (((1,), (0,)), ((), ())), preferred_element_type=jnp.float32)


def folds(width):
    return 4 if width % 512 == 0 else 1


def slab_rows(width):
    return max(SLAB, folds(width) * SLOT)


def stack(slabs):
    return jnp.concatenate([ref[...].astype(jnp.float32) for ref in slabs], 0).astype(jnp.bfloat16)


def pieces(width):
    size = width // folds(width)
    return [(p, slice(p * size, (p + 1) * size)) for p in range(folds(width))]


def iota(shape, dim):
    return lax.broadcasted_iota(jnp.int32, shape, dim)


def job_copies(jobs, half, up_hbm, targets, sems):
    q = lax.axis_index("tensor")
    copies = []
    for i, job in enumerate(jobs):
        start = (q ^ (job // 2)) * 2 * half + (job % 2) * half
        at = pl.ds(pl.multiple_of(start, 128), half)
        copies.append(pltpu.make_async_copy(up_hbm.at[at, :], targets[i], sems.at[i]))
    return copies


def select_kernel(n, ids_hbm, route_hbm, tok_hbm, comb_ref, *refs):
    slabs, (ids_ref, route_ref, tok_ref, sems) = refs[:n], refs[n:]
    inputs = [
        pltpu.make_async_copy(source, target, sems.at[i])
        for i, (source, target) in enumerate(
            ((ids_hbm, ids_ref), (route_hbm, route_ref), (tok_hbm, tok_ref))
        )
    ]
    for copy in inputs:
        copy.start()
    for copy in inputs:
        copy.wait()
    me = lax.axis_index("expert")
    replicas = n // E_W
    ids, route, tok = ids_ref[...], route_ref[...], tok_ref[...]
    count = tok.shape[0]
    before = (iota((count, count), 0) <= iota((count, count), 1)).astype(jnp.bfloat16)
    slot = iota((SLAB, count), 0).astype(jnp.float32)
    width = tok.shape[1]
    tall = slab_rows(width)
    row = iota((tall, count), 0).astype(jnp.float32)
    members, positions = [], []
    for k in range(n):
        hit = ids == (me ^ k) // replicas
        member = jnp.sum(jnp.where(hit, 1.0, 0.0), axis=0, keepdims=True)
        weight = jnp.sum(jnp.where(hit, route, 0.0), axis=0, keepdims=True)
        member = jnp.broadcast_to(member, (SLAB, count))
        position = dot(member.astype(jnp.bfloat16), before) - 1.0
        placed = jnp.where(position == slot, member, 0.0)
        comb_ref[k * SLAB : (k + 1) * SLAB, :] = placed * weight
        members.append(jnp.broadcast_to(member[:1], (tall, count)))
        positions.append(jnp.broadcast_to(position[:1], (tall, count)))
    total = None
    for p, piece in pieces(width):
        take = [
            jnp.where(position + float(p * SLOT) == row, member, 0.0)
            for position, member in zip(positions, members)
        ]
        part = dot(jnp.concatenate(take, 0).astype(jnp.bfloat16), tok[:, piece])
        total = part if total is None else total + part
    for k in range(n):
        slabs[k][...] = total[k * tall : (k + 1) * tall].astype(jnp.bfloat16)


def select(n, ids, route, tokens):
    count, width = tokens.shape
    out = pl.pallas_call(
        functools.partial(select_kernel, n),
        out_shape=[VMEM((n * SLAB, count), jnp.float32)]
        + [VMEM((slab_rows(width), width // folds(width)), jnp.bfloat16)] * n,
        in_specs=[spec(HBM)] * 3,
        out_specs=[spec(VMEM)] * (n + 1),
        scratch_shapes=[
            VMEM(ids.shape, ids.dtype),
            VMEM(route.shape, route.dtype),
            VMEM(tokens.shape, tokens.dtype),
            DMA((3,)),
        ],
        compiler_params=limit(4),
        cost_estimate=lasts(40),
        name="select",
    )(ids, route, tokens)
    return out[0], out[1:]


def compact_kernel(n, *refs):
    slabs, rows_ref = refs[:n], refs[-1]
    full = stack(slabs)
    tall, width = slabs[0].shape[0], rows_ref.shape[1]
    col = iota((n * SLOT, n * tall), 1)
    for p, piece in pieces(width):
        s = col % tall - p * SLOT
        take = (iota((n * SLOT, n * tall), 0) == col // tall * SLOT + s) & (s >= 0) & (s < SLOT)
        rows_ref[:, piece] = dot(take.astype(jnp.bfloat16), full).astype(jnp.bfloat16)


def compact(width, slabs, after):
    n = len(slabs)
    return pl.pallas_call(
        functools.partial(compact_kernel, n),
        out_shape=VMEM((n * SLOT, width), jnp.bfloat16),
        in_specs=[spec(VMEM)] * (n + 1),
        out_specs=spec(VMEM),
        compiler_params=limit(4),
        name="compact",
    )(*slabs, after)


def chunk(weight_ref, k, width, side, half, tile):
    start = (lax.axis_index("tensor") ^ k) * width + side
    return weight_ref[pl.ds(pl.multiple_of(start, 128), half), tile]


def tiles(n):
    return [slice(at, at + min(TILE, n)) for at in range(0, n, min(TILE, n))]


def fetch_kernel(jobs, half, order_ref, up_hbm, *refs):
    held, sems = refs[:-1], refs[-1]
    copies = job_copies(jobs, half, up_hbm, held, sems)
    for copy in copies:
        copy.start()
    for copy in copies:
        copy.wait()


def fetch(jobs, half, order, w_up):
    shape = (half, w_up.shape[1])
    return pl.pallas_call(
        functools.partial(fetch_kernel, jobs, half),
        out_shape=[VMEM(shape, jnp.bfloat16)] * len(jobs),
        in_specs=[spec(VMEM), spec(HBM)],
        out_specs=[spec(VMEM)] * len(jobs),
        scratch_shapes=[DMA((len(jobs),))],
        compiler_params=limit(2),
        cost_estimate=lasts(0.2),
        name="fetch",
    )(order, w_up)


def own_kernel(jobs, n, rows_ref, comb_ref, up_low, up_high, up_hbm, sum_u, mix_ref, *refs):
    held, sems = refs[:-1], refs[-1]
    half = rows_ref.shape[1] // 2
    copies = job_copies(jobs, half, up_hbm, held, sems)
    for copy in copies:
        copy.start()
    low, high = rows_ref[:, :half], rows_ref[:, half:]
    steps = tiles(sum_u.shape[1])
    done = 0
    for i, tile in enumerate(steps):
        sum_u[:, tile] = dot(low, up_low[:, tile]) + dot(high, up_high[:, tile])
        while done < len(copies) and done * len(steps) < (i + 1) * len(copies):
            copies[done].wait()
            done += 1
    comb = comb_ref[...].T
    count, width = comb.shape[0], rows_ref.shape[1]
    tall = slab_rows(width)
    row, col = iota((n * SLAB, n * tall), 0), iota((n * SLAB, n * tall), 1)
    for i in range(3):
        term = comb.astype(jnp.bfloat16)
        comb = comb - term.astype(jnp.float32)
        for p, _ in pieces(width):
            s = col % tall - p * SLOT
            take = (row == col // tall * SLAB + s) & (s >= 0) & (s < SLOT)
            part = dot(term, take.astype(jnp.bfloat16)).astype(jnp.bfloat16)
            mix_ref[i, p * count : (p + 1) * count, :] = part
    for copy in copies[done:]:
        copy.wait()


def own(jobs, axis, rows, comb, held, w_up):
    (m, width), n = rows.shape, w_up.shape[1]
    mix = (3, folds(width) * comb.shape[1], axis * slab_rows(width))
    return pl.pallas_call(
        functools.partial(own_kernel, jobs, axis),
        out_shape=[VMEM((m, n), jnp.float32), VMEM(mix, jnp.bfloat16)]
        + [VMEM((width // 2, n), jnp.bfloat16)] * len(jobs),
        in_specs=[spec(VMEM)] * 4 + [spec(HBM)],
        out_specs=[spec(VMEM)] * (2 + len(jobs)),
        scratch_shapes=[DMA((len(jobs),))],
        compiler_params=limit(2),
        cost_estimate=lasts(0.2),
        name="own",
    )(rows, comb, *held, w_up)


def down_copy(k, down_hbm, target, sem):
    width = target.shape[1]
    q = lax.axis_index("tensor")
    at = pl.ds(pl.multiple_of((q ^ k) * width, 128), width)
    return pltpu.make_async_copy(down_hbm.at[:, at], target, sem)


def rest_kernel(outs, first, *refs):
    parts = len(outs) + 2
    rows, refs = refs[:parts], refs[parts:]
    held, refs = refs[: first - 2], refs[first - 2 :]
    start_u, gate_ref, up_hbm, down_hbm, hidden_ref = refs[:5]
    sent, refs = refs[5 : 5 + len(outs)], refs[5 + len(outs) :]
    late, down2, sum_g, late_sems, down_sems = refs
    width = rows[0].shape[1]
    half = width // 2
    slots, deep = down2.shape[:2]
    n = hidden_ref.shape[1]
    wide = min(WIDE, n)
    deep_gate = 256 if width % 256 == 0 else 128
    cuts = n // deep
    jobs = range(first, 2 * parts)
    lates = job_copies(jobs, half, up_hbm, [late.at[i] for i in range(len(jobs))], late_sems)
    downs = []
    for i in range(cuts * len(outs)):
        rows_at, slot = down_hbm.at[pl.ds(i % cuts * deep, deep), :], i % slots
        downs.append(down_copy(outs[i // cuts], rows_at, down2.at[slot], down_sems.at[slot]))
    for copy in lates:
        copy.start()
    ups = list(held) + [late.at[i] for i in range(len(jobs))]

    def gate_part(step):
        at = pl.ds(pl.multiple_of(step * wide, 128), wide)
        total = None
        for k in range(parts):
            for side in range(0, width, deep_gate):
                row = rows[k][:, side : side + deep_gate]
                part = dot(row, chunk(gate_ref, k, width, side, deep_gate, at))
                total = part if total is None else total + part
        sum_g[:, at] = total

    middle = n // wide // 2
    pl.loop(0, middle)(gate_part)
    for copy in downs[:slots]:
        copy.start()
    pl.loop(middle, n // wide)(gate_part)
    for copy in lates:
        copy.wait()

    @pl.loop(0, n // wide)
    def _(step):
        at = pl.ds(pl.multiple_of(step * wide, 128), wide)
        total = start_u[:, at]
        for k in range(1, parts):
            total += dot(rows[k][:, :half], ups[2 * k - 2][:, at])
            total += dot(rows[k][:, half:], ups[2 * k - 1][:, at])
        gate = sum_g[:, at]
        hidden_ref[:, at] = (gate / (1.0 + jnp.exp(-gate)) * total).astype(jnp.bfloat16)

    for i in range(len(outs)):
        for j in range(cuts):
            piece = cuts * i + j
            downs[piece].wait()

            @pl.loop(0, 2)
            def _(step):
                at = pl.ds(pl.multiple_of(step * half, 128), half)
                mid = hidden_ref[:, j * deep : (j + 1) * deep]
                part = dot(mid, down2[piece % slots, :, at])
                if j > 0:
                    part += sum_g[:, at]
                if j < cuts - 1:
                    sum_g[:, at] = part
                else:
                    sent[i][:, at] = part.astype(jnp.bfloat16)

            if piece + slots < len(downs):
                downs[piece + slots].start()


def rest(outs, rows, held, sum_u, w_gate, w_up, w_down):
    m, n = sum_u.shape
    width = rows[0].shape[1]
    cuts = 2 if n % 256 == 0 else 1
    first = 2 + len(held)
    late = max(1, 2 * len(rows) - first)
    return pl.pallas_call(
        functools.partial(rest_kernel, outs, first),
        out_shape=[VMEM((m, n), jnp.bfloat16)] + [VMEM((m, width), jnp.bfloat16)] * len(outs),
        in_specs=[spec(VMEM)] * (len(rows) + len(held) + 2) + [spec(HBM)] * 2,
        out_specs=[spec(VMEM)] * (1 + len(outs)),
        scratch_shapes=[
            VMEM((late, width // 2, n), jnp.bfloat16),
            VMEM((DOWNS, n // cuts, width), jnp.bfloat16),
            VMEM((m, max(n, width)), jnp.float32),
            DMA((late,)),
            DMA((DOWNS,)),
        ],
        compiler_params=limit(22),
        cost_estimate=lasts(10),
        name="rest",
    )(*rows, *held, sum_u, w_gate, w_up, w_down)


def near_kernel(hidden_ref, down_hbm, sent, next_ref, buf, total, sems):
    cuts, deep = buf.shape[:2]
    copies = []
    for j in range(cuts):
        rows_at = down_hbm.at[pl.ds(j * deep, deep), :]
        copies.append(down_copy(1, rows_at, buf.at[j], sems.at[j]))
    for j in range(cuts):
        at = pl.ds(j * deep, deep)
        copies.append(down_copy(0, down_hbm.at[at, :], next_ref.at[at, :], sems.at[cuts + j]))
    for copy in copies:
        copy.start()
    for j in range(cuts):
        copies[j].wait()
        mid = hidden_ref[:, j * deep : (j + 1) * deep]
        for tile in tiles(sent.shape[1]):
            part = dot(mid, buf[j, :, tile])
            if j > 0:
                part += total[:, tile]
            if j < cuts - 1:
                total[:, tile] = part
            else:
                sent[:, tile] = part.astype(jnp.bfloat16)
    for copy in copies[cuts:]:
        copy.wait()


def near(width, hidden, w_down):
    m, n = hidden.shape
    cuts = 2 if n % 256 == 0 else 1
    return pl.pallas_call(
        near_kernel,
        out_shape=[VMEM((m, width), jnp.bfloat16), VMEM((n, width), jnp.bfloat16)],
        in_specs=[spec(VMEM), spec(HBM)],
        out_specs=[spec(VMEM)] * 2,
        scratch_shapes=[
            VMEM((cuts, n // cuts, width), jnp.bfloat16),
            VMEM((m, width), jnp.float32),
            DMA((2 * cuts,)),
        ],
        compiler_params=limit(12),
        cost_estimate=lasts(4),
        name="near",
    )(hidden, w_down)


def keep_kernel(hidden_ref, weight_ref, total_ref):
    total_ref[...] = dot(hidden_ref[...], weight_ref[...])


def keep(hidden, weight):
    m, width = hidden.shape[0], weight.shape[1]
    return pl.pallas_call(
        keep_kernel,
        out_shape=VMEM((m, width), jnp.float32),
        in_specs=[spec(VMEM)] * 2,
        out_specs=spec(VMEM),
        compiler_params=limit(4),
        cost_estimate=lasts(1),
        name="keep",
    )(hidden, weight)


def gather_kernel(total_ref, *refs):
    terms, sum_ref = refs[:-1], refs[-1]
    total = total_ref[...]
    for term in terms:
        total = total + term[...].astype(jnp.float32)
    sum_ref[...] = total


def gather(total, terms):
    return pl.pallas_call(
        gather_kernel,
        out_shape=VMEM(total.shape, jnp.float32),
        in_specs=[spec(VMEM)] * (1 + len(terms)),
        out_specs=spec(VMEM),
        compiler_params=limit(4),
        cost_estimate=lasts(2),
        name="gather",
    )(total, *terms)


def add_kernel(n, total_ref, *refs):
    terms, slabs = refs[:-n], refs[-n:]
    total = total_ref[...]
    for term in terms:
        total = total + term[...].astype(jnp.float32)
    total = total.astype(jnp.bfloat16)
    width = total.shape[1]
    tall = slab_rows(width)
    row, col = iota((n * tall, n * SLOT), 0), iota((n * tall, n * SLOT), 1)
    full = None
    for p, piece in pieces(width):
        s = row % tall - p * SLOT
        take = (col == row // tall * SLOT + s) & (s >= 0) & (s < SLOT)
        part = dot(take.astype(jnp.bfloat16), total[:, piece])
        full = part if full is None else full + part
    for k in range(n):
        slabs[k][...] = full[k * tall : (k + 1) * tall].astype(jnp.bfloat16)


def add(n, total, terms):
    width = total.shape[1]
    return pl.pallas_call(
        functools.partial(add_kernel, n),
        out_shape=[VMEM((slab_rows(width), width // folds(width)), jnp.bfloat16)] * n,
        in_specs=[spec(VMEM)] * (1 + len(terms)),
        out_specs=[spec(VMEM)] * n,
        compiler_params=limit(4),
        name="add",
    )(total, *terms)


def combine_kernel(mix_ref, *refs):
    slabs, out_ref = refs[:-1], refs[-1]
    full = stack(slabs)
    count, width = out_ref.shape
    total = dot(mix_ref[0], full) + (dot(mix_ref[1], full) + dot(mix_ref[2], full))
    for p, piece in pieces(width):
        out_ref[:, piece] = total[p * count : (p + 1) * count].astype(jnp.bfloat16)


def combine(width, mix, slabs):
    n = len(slabs)
    return pl.pallas_call(
        combine_kernel,
        out_shape=jax.ShapeDtypeStruct((mix.shape[1] // folds(width), width), jnp.bfloat16),
        in_specs=[spec(VMEM)] * (n + 1),
        out_specs=spec(VMEM),
        compiler_params=limit(4),
        name="combine",
    )(mix, *slabs)


def swap(x, axis, k):
    size = lax.axis_size(axis)
    return lax.ppermute(x, axis, [(i, i ^ k) for i in range(size)])


def per_device(*args):
    tokens, ids, route, w_up, w_down = (
        pltpu.with_memory_space_constraint(x, HBM)
        for x in (args[0], args[1].T, args[2].T, args[4], args[5])
    )
    w_gate = args[3]
    n, parts = lax.axis_size("expert"), lax.axis_size("tensor")
    width = tokens.shape[1]
    comb, slabs = select(n, ids, route, tokens)
    slabs = [slabs[0]] + [swap(slabs[k], "expert", k) for k in range(1, n)]
    held = fetch(range(FETCH), width // 2, comb, w_up)
    mine = compact(width, slabs, held[-1])
    rows = [mine] + [swap(mine, "tensor", k) for k in range(1, parts)]
    sum_u, mix, *more = own(range(FETCH, OWN), n, mine, comb, held[:2], w_up)
    held = [*held[2:], *more]
    far = list(range(parts - 1, 1, -1))
    hidden, *sent = rest(far, rows, held, sum_u, w_gate, w_up, w_down)
    terms = [swap(x, "tensor", k) for k, x in zip(far, sent)]
    sent, weight0 = near(width, hidden, w_down)
    last = swap(sent, "tensor", 1)
    total = gather(keep(hidden, weight0), terms)
    back = add(n, total, [last])
    back = [back[0]] + [swap(back[k], "expert", k) for k in range(1, n)]
    return combine(width, mix, back)


def solution(mesh):
    return jax.shard_map(
        per_device,
        mesh=mesh,
        in_specs=(
            P(("groups", "expert"), "tensor"),
            P(("groups", "expert"), None),
            P(("groups", "expert"), None),
            P(None, ("expert", "tensor")),
            P(None, ("expert", "tensor")),
            P(("expert", "tensor"), None),
        ),
        out_specs=P(("groups", "expert"), "tensor"),
        check_vma=False,
    )
```

```python
import functools

import jax
import jax.numpy as jnp
from jax import lax
from jax.experimental import pallas as pl
from jax.experimental.pallas import tpu as pltpu
from jax.sharding import PartitionSpec as P

E_W = 4
SLOT = 10
SLAB = 16
FETCH = 2
OWN = 4
DOWNS = 4
TILE = 512
WIDE = 512
MICRO = 1_150_000_000
MIB = 1 << 20
VMEM = pltpu.VMEM
HBM = pltpu.HBM
DMA = pltpu.SemaphoreType.DMA


def spec(space):
    return pl.BlockSpec(memory_space=space)


def limit(mib):
    return pltpu.CompilerParams(vmem_limit_bytes=mib * MIB)


def lasts(micros):
    return pl.CostEstimate(flops=int(micros * MICRO), bytes_accessed=0, transcendentals=0)


def dot(a, b):
    return lax.dot_general(a, b, (((1,), (0,)), ((), ())), preferred_element_type=jnp.float32)


def folds(width):
    return 4 if width % 512 == 0 else 1


def slab_rows(width):
    return max(SLAB, folds(width) * SLOT)


def stack(slabs):
    return jnp.concatenate([ref[...].astype(jnp.float32) for ref in slabs], 0).astype(jnp.bfloat16)


def pieces(width):
    size = width // folds(width)
    return [(p, slice(p * size, (p + 1) * size)) for p in range(folds(width))]


def iota(shape, dim):
    return lax.broadcasted_iota(jnp.int32, shape, dim)


def job_copies(jobs, half, up_hbm, targets, sems):
    q = lax.axis_index("tensor")
    copies = []
    for i, job in enumerate(jobs):
        start = (q ^ (job // 2)) * 2 * half + (job % 2) * half
        at = pl.ds(pl.multiple_of(start, 128), half)
        copies.append(pltpu.make_async_copy(up_hbm.at[at, :], targets[i], sems.at[i]))
    return copies


def select_kernel(n, ids_hbm, route_hbm, tok_hbm, comb_ref, *refs):
    slabs, (ids_ref, route_ref, tok_ref, sems) = refs[:n], refs[n:]
    inputs = [
        pltpu.make_async_copy(source, target, sems.at[i])
        for i, (source, target) in enumerate(
            ((ids_hbm, ids_ref), (route_hbm, route_ref), (tok_hbm, tok_ref))
        )
    ]
    for copy in inputs:
        copy.start()
    for copy in inputs:
        copy.wait()
    me = lax.axis_index("expert")
    replicas = n // E_W
    ids, route, tok = ids_ref[...], route_ref[...], tok_ref[...]
    count = tok.shape[0]
    before = (iota((count, count), 0) <= iota((count, count), 1)).astype(jnp.bfloat16)
    slot = iota((SLAB, count), 0).astype(jnp.float32)
    width = tok.shape[1]
    tall = slab_rows(width)
    row = iota((tall, count), 0).astype(jnp.float32)
    members, positions = [], []
    for k in range(n):
        hit = ids == (me ^ k) // replicas
        member = jnp.sum(jnp.where(hit, 1.0, 0.0), axis=0, keepdims=True)
        weight = jnp.sum(jnp.where(hit, route, 0.0), axis=0, keepdims=True)
        member = jnp.broadcast_to(member, (SLAB, count))
        position = dot(member.astype(jnp.bfloat16), before) - 1.0
        placed = jnp.where(position == slot, member, 0.0)
        comb_ref[k * SLAB : (k + 1) * SLAB, :] = placed * weight
        members.append(jnp.broadcast_to(member[:1], (tall, count)))
        positions.append(jnp.broadcast_to(position[:1], (tall, count)))
    total = None
    for p, piece in pieces(width):
        take = [
            jnp.where(position + float(p * SLOT) == row, member, 0.0)
            for position, member in zip(positions, members)
        ]
        part = dot(jnp.concatenate(take, 0).astype(jnp.bfloat16), tok[:, piece])
        total = part if total is None else total + part
    for k in range(n):
        slabs[k][...] = total[k * tall : (k + 1) * tall].astype(jnp.bfloat16)


def select(n, ids, route, tokens):
    count, width = tokens.shape
    out = pl.pallas_call(
        functools.partial(select_kernel, n),
        out_shape=[VMEM((n * SLAB, count), jnp.float32)]
        + [VMEM((slab_rows(width), width // folds(width)), jnp.bfloat16)] * n,
        in_specs=[spec(HBM)] * 3,
        out_specs=[spec(VMEM)] * (n + 1),
        scratch_shapes=[
            VMEM(ids.shape, ids.dtype),
            VMEM(route.shape, route.dtype),
            VMEM(tokens.shape, tokens.dtype),
            DMA((3,)),
        ],
        compiler_params=limit(4),
        cost_estimate=lasts(40),
        name="select",
    )(ids, route, tokens)
    return out[0], out[1:]


def compact_kernel(n, *refs):
    slabs, rows_ref = refs[:n], refs[-1]
    full = stack(slabs)
    tall, width = slabs[0].shape[0], rows_ref.shape[1]
    col = iota((n * SLOT, n * tall), 1)
    for p, piece in pieces(width):
        s = col % tall - p * SLOT
        take = (iota((n * SLOT, n * tall), 0) == col // tall * SLOT + s) & (s >= 0) & (s < SLOT)
        rows_ref[:, piece] = dot(take.astype(jnp.bfloat16), full).astype(jnp.bfloat16)


def compact(width, slabs, after):
    n = len(slabs)
    return pl.pallas_call(
        functools.partial(compact_kernel, n),
        out_shape=VMEM((n * SLOT, width), jnp.bfloat16),
        in_specs=[spec(VMEM)] * (n + 1),
        out_specs=spec(VMEM),
        compiler_params=limit(4),
        name="compact",
    )(*slabs, after)


def chunk(weight_ref, k, width, side, half, tile):
    start = (lax.axis_index("tensor") ^ k) * width + side
    return weight_ref[pl.ds(pl.multiple_of(start, 128), half), tile]


def tiles(n):
    return [slice(at, at + min(TILE, n)) for at in range(0, n, min(TILE, n))]


def fetch_kernel(jobs, half, order_ref, up_hbm, *refs):
    held, sems = refs[:-1], refs[-1]
    copies = job_copies(jobs, half, up_hbm, held, sems)
    for copy in copies:
        copy.start()
    for copy in copies:
        copy.wait()


def fetch(jobs, half, order, w_up):
    shape = (half, w_up.shape[1])
    return pl.pallas_call(
        functools.partial(fetch_kernel, jobs, half),
        out_shape=[VMEM(shape, jnp.bfloat16)] * len(jobs),
        in_specs=[spec(VMEM), spec(HBM)],
        out_specs=[spec(VMEM)] * len(jobs),
        scratch_shapes=[DMA((len(jobs),))],
        compiler_params=limit(2),
        cost_estimate=lasts(0.2),
        name="fetch",
    )(order, w_up)


def own_kernel(jobs, n, rows_ref, comb_ref, up_low, up_high, up_hbm, sum_u, mix_ref, *refs):
    held, sems = refs[:-1], refs[-1]
    half = rows_ref.shape[1] // 2
    copies = job_copies(jobs, half, up_hbm, held, sems)
    for copy in copies:
        copy.start()
    low, high = rows_ref[:, :half], rows_ref[:, half:]
    steps = tiles(sum_u.shape[1])
    done = 0
    for i, tile in enumerate(steps):
        sum_u[:, tile] = dot(low, up_low[:, tile]) + dot(high, up_high[:, tile])
        while done < len(copies) and done * len(steps) < (i + 1) * len(copies):
            copies[done].wait()
            done += 1
    comb = comb_ref[...].T
    count, width = comb.shape[0], rows_ref.shape[1]
    tall = slab_rows(width)
    row, col = iota((n * SLAB, n * tall), 0), iota((n * SLAB, n * tall), 1)
    for i in range(3):
        term = comb.astype(jnp.bfloat16)
        comb = comb - term.astype(jnp.float32)
        for p, _ in pieces(width):
            s = col % tall - p * SLOT
            take = (row == col // tall * SLAB + s) & (s >= 0) & (s < SLOT)
            part = dot(term, take.astype(jnp.bfloat16)).astype(jnp.bfloat16)
            mix_ref[i, p * count : (p + 1) * count, :] = part
    for copy in copies[done:]:
        copy.wait()


def own(jobs, axis, rows, comb, held, w_up):
    (m, width), n = rows.shape, w_up.shape[1]
    mix = (3, folds(width) * comb.shape[1], axis * slab_rows(width))
    return pl.pallas_call(
        functools.partial(own_kernel, jobs, axis),
        out_shape=[VMEM((m, n), jnp.float32), VMEM(mix, jnp.bfloat16)]
        + [VMEM((width // 2, n), jnp.bfloat16)] * len(jobs),
        in_specs=[spec(VMEM)] * 4 + [spec(HBM)],
        out_specs=[spec(VMEM)] * (2 + len(jobs)),
        scratch_shapes=[DMA((len(jobs),))],
        compiler_params=limit(2),
        cost_estimate=lasts(0.2),
        name="own",
    )(rows, comb, *held, w_up)


def second_kernel(rows_ref, sum_u, up_low, up_high, out_ref):
    half = rows_ref.shape[1] // 2
    for tile in tiles(sum_u.shape[1]):
        part = dot(rows_ref[:, :half], up_low[:, tile]) + dot(rows_ref[:, half:], up_high[:, tile])
        out_ref[:, tile] = sum_u[:, tile] + part


def second(rows, sum_u, held):
    return pl.pallas_call(
        second_kernel,
        out_shape=VMEM(sum_u.shape, jnp.float32),
        in_specs=[spec(VMEM)] * 4,
        out_specs=spec(VMEM),
        compiler_params=limit(2),
        cost_estimate=lasts(1),
        name="second",
    )(rows, sum_u, *held)


def down_copy(k, down_hbm, target, sem):
    width = target.shape[1]
    q = lax.axis_index("tensor")
    at = pl.ds(pl.multiple_of((q ^ k) * width, 128), width)
    return pltpu.make_async_copy(down_hbm.at[:, at], target, sem)


def rest_kernel(outs, first, *refs):
    parts = len(outs) + 2
    rows, refs = refs[:parts], refs[parts:]
    held, refs = refs[: first - 4], refs[first - 4 :]
    start_u, gate_ref, up_hbm, down_hbm, hidden_ref = refs[:5]
    sent, refs = refs[5 : 5 + len(outs)], refs[5 + len(outs) :]
    late, down2, sum_g, late_sems, down_sems = refs
    width = rows[0].shape[1]
    half = width // 2
    slots, deep = down2.shape[:2]
    n = hidden_ref.shape[1]
    wide = min(WIDE, n)
    deep_gate = 256 if width % 256 == 0 else 128
    cuts = n // deep
    jobs = range(first, 2 * parts)
    lates = job_copies(jobs, half, up_hbm, [late.at[i] for i in range(len(jobs))], late_sems)
    downs = []
    for i in range(cuts * len(outs)):
        rows_at, slot = down_hbm.at[pl.ds(i % cuts * deep, deep), :], i % slots
        downs.append(down_copy(outs[i // cuts], rows_at, down2.at[slot], down_sems.at[slot]))
    for copy in lates:
        copy.start()
    ups = list(held) + [late.at[i] for i in range(len(jobs))]

    def gate_part(step):
        at = pl.ds(pl.multiple_of(step * wide, 128), wide)
        total = None
        for k in range(parts):
            for side in range(0, width, deep_gate):
                row = rows[k][:, side : side + deep_gate]
                part = dot(row, chunk(gate_ref, k, width, side, deep_gate, at))
                total = part if total is None else total + part
        sum_g[:, at] = total

    middle = n // wide // 2
    pl.loop(0, middle)(gate_part)
    for copy in downs[:slots]:
        copy.start()
    pl.loop(middle, n // wide)(gate_part)
    for copy in lates:
        copy.wait()

    @pl.loop(0, n // wide)
    def _(step):
        at = pl.ds(pl.multiple_of(step * wide, 128), wide)
        total = start_u[:, at]
        for k in range(2, parts):
            total += dot(rows[k][:, :half], ups[2 * k - 4][:, at])
            total += dot(rows[k][:, half:], ups[2 * k - 3][:, at])
        gate = sum_g[:, at]
        hidden_ref[:, at] = (gate / (1.0 + jnp.exp(-gate)) * total).astype(jnp.bfloat16)

    for i in range(len(outs)):
        for j in range(cuts):
            piece = cuts * i + j
            downs[piece].wait()

            @pl.loop(0, 2)
            def _(step):
                at = pl.ds(pl.multiple_of(step * half, 128), half)
                mid = hidden_ref[:, j * deep : (j + 1) * deep]
                part = dot(mid, down2[piece % slots, :, at])
                if j > 0:
                    part += sum_g[:, at]
                if j < cuts - 1:
                    sum_g[:, at] = part
                else:
                    sent[i][:, at] = part.astype(jnp.bfloat16)

            if piece + slots < len(downs):
                downs[piece + slots].start()


def rest(outs, rows, held, sum_u, w_gate, w_up, w_down):
    m, n = sum_u.shape
    width = rows[0].shape[1]
    cuts = 2 if n % 256 == 0 else 1
    first = 4 + len(held)
    late = max(1, 2 * len(rows) - first)
    return pl.pallas_call(
        functools.partial(rest_kernel, outs, first),
        out_shape=[VMEM((m, n), jnp.bfloat16)] + [VMEM((m, width), jnp.bfloat16)] * len(outs),
        in_specs=[spec(VMEM)] * (len(rows) + len(held) + 2) + [spec(HBM)] * 2,
        out_specs=[spec(VMEM)] * (1 + len(outs)),
        scratch_shapes=[
            VMEM((late, width // 2, n), jnp.bfloat16),
            VMEM((DOWNS, n // cuts, width), jnp.bfloat16),
            VMEM((m, max(n, width)), jnp.float32),
            DMA((late,)),
            DMA((DOWNS,)),
        ],
        compiler_params=limit(26),
        cost_estimate=lasts(10),
        name="rest",
    )(*rows, *held, sum_u, w_gate, w_up, w_down)


def near_kernel(hidden_ref, down_hbm, sent, next_ref, buf, total, sems):
    cuts, deep = buf.shape[:2]
    copies = []
    for j in range(cuts):
        rows_at = down_hbm.at[pl.ds(j * deep, deep), :]
        copies.append(down_copy(1, rows_at, buf.at[j], sems.at[j]))
    for j in range(cuts):
        at = pl.ds(j * deep, deep)
        copies.append(down_copy(0, down_hbm.at[at, :], next_ref.at[at, :], sems.at[cuts + j]))
    for copy in copies:
        copy.start()
    for j in range(cuts):
        copies[j].wait()
        mid = hidden_ref[:, j * deep : (j + 1) * deep]
        for tile in tiles(sent.shape[1]):
            part = dot(mid, buf[j, :, tile])
            if j > 0:
                part += total[:, tile]
            if j < cuts - 1:
                total[:, tile] = part
            else:
                sent[:, tile] = part.astype(jnp.bfloat16)
    for copy in copies[cuts:]:
        copy.wait()


def near(width, hidden, w_down):
    m, n = hidden.shape
    cuts = 2 if n % 256 == 0 else 1
    return pl.pallas_call(
        near_kernel,
        out_shape=[VMEM((m, width), jnp.bfloat16), VMEM((n, width), jnp.bfloat16)],
        in_specs=[spec(VMEM), spec(HBM)],
        out_specs=[spec(VMEM)] * 2,
        scratch_shapes=[
            VMEM((cuts, n // cuts, width), jnp.bfloat16),
            VMEM((m, width), jnp.float32),
            DMA((2 * cuts,)),
        ],
        compiler_params=limit(12),
        cost_estimate=lasts(4),
        name="near",
    )(hidden, w_down)


def keep_kernel(hidden_ref, weight_ref, total_ref):
    total_ref[...] = dot(hidden_ref[...], weight_ref[...])


def keep(hidden, weight):
    m, width = hidden.shape[0], weight.shape[1]
    return pl.pallas_call(
        keep_kernel,
        out_shape=VMEM((m, width), jnp.float32),
        in_specs=[spec(VMEM)] * 2,
        out_specs=spec(VMEM),
        compiler_params=limit(4),
        cost_estimate=lasts(1),
        name="keep",
    )(hidden, weight)


def gather_kernel(total_ref, *refs):
    terms, sum_ref = refs[:-1], refs[-1]
    total = total_ref[...]
    for term in terms:
        total = total + term[...].astype(jnp.float32)
    sum_ref[...] = total


def gather(total, terms):
    return pl.pallas_call(
        gather_kernel,
        out_shape=VMEM(total.shape, jnp.float32),
        in_specs=[spec(VMEM)] * (1 + len(terms)),
        out_specs=spec(VMEM),
        compiler_params=limit(4),
        cost_estimate=lasts(2),
        name="gather",
    )(total, *terms)


def add_kernel(n, total_ref, *refs):
    terms, slabs = refs[:-n], refs[-n:]
    total = total_ref[...]
    for term in terms:
        total = total + term[...].astype(jnp.float32)
    total = total.astype(jnp.bfloat16)
    width = total.shape[1]
    tall = slab_rows(width)
    row, col = iota((n * tall, n * SLOT), 0), iota((n * tall, n * SLOT), 1)
    full = None
    for p, piece in pieces(width):
        s = row % tall - p * SLOT
        take = (col == row // tall * SLOT + s) & (s >= 0) & (s < SLOT)
        part = dot(take.astype(jnp.bfloat16), total[:, piece])
        full = part if full is None else full + part
    for k in range(n):
        slabs[k][...] = full[k * tall : (k + 1) * tall].astype(jnp.bfloat16)


def add(n, total, terms):
    width = total.shape[1]
    return pl.pallas_call(
        functools.partial(add_kernel, n),
        out_shape=[VMEM((slab_rows(width), width // folds(width)), jnp.bfloat16)] * n,
        in_specs=[spec(VMEM)] * (1 + len(terms)),
        out_specs=[spec(VMEM)] * n,
        compiler_params=limit(4),
        name="add",
    )(total, *terms)


def combine_kernel(mix_ref, *refs):
    slabs, out_ref = refs[:-1], refs[-1]
    full = stack(slabs)
    count, width = out_ref.shape
    total = dot(mix_ref[0], full) + (dot(mix_ref[1], full) + dot(mix_ref[2], full))
    for p, piece in pieces(width):
        out_ref[:, piece] = total[p * count : (p + 1) * count].astype(jnp.bfloat16)


def combine(width, mix, slabs):
    n = len(slabs)
    return pl.pallas_call(
        combine_kernel,
        out_shape=jax.ShapeDtypeStruct((mix.shape[1] // folds(width), width), jnp.bfloat16),
        in_specs=[spec(VMEM)] * (n + 1),
        out_specs=spec(VMEM),
        compiler_params=limit(4),
        name="combine",
    )(mix, *slabs)


def swap(x, axis, k):
    size = lax.axis_size(axis)
    return lax.ppermute(x, axis, [(i, i ^ k) for i in range(size)])


def per_device(*args):
    tokens, ids, route, w_up, w_down = (
        pltpu.with_memory_space_constraint(x, HBM)
        for x in (args[0], args[1].T, args[2].T, args[4], args[5])
    )
    w_gate = args[3]
    n, parts = lax.axis_size("expert"), lax.axis_size("tensor")
    width = tokens.shape[1]
    comb, slabs = select(n, ids, route, tokens)
    slabs = [slabs[0]] + [swap(slabs[k], "expert", k) for k in range(1, n)]
    held = fetch(range(FETCH), width // 2, comb, w_up)
    mine = compact(width, slabs, held[-1])
    rows = [mine] + [swap(mine, "tensor", k) for k in range(1, parts)]
    sum_u, mix, *more = own(range(FETCH, OWN), n, mine, comb, held[:2], w_up)
    held = [*held[2:], *more]
    sum_u = second(rows[1], sum_u, held[:2])
    held = held[2:]
    far = list(range(parts - 1, 1, -1))
    hidden, *sent = rest(far, rows, held, sum_u, w_gate, w_up, w_down)
    terms = [swap(x, "tensor", k) for k, x in zip(far, sent)]
    sent, weight0 = near(width, hidden, w_down)
    last = swap(sent, "tensor", 1)
    total = gather(keep(hidden, weight0), terms)
    back = add(n, total, [last])
    back = [back[0]] + [swap(back[k], "expert", k) for k in range(1, n)]
    return combine(width, mix, back)


def solution(mesh):
    return jax.shard_map(
        per_device,
        mesh=mesh,
        in_specs=(
            P(("groups", "expert"), "tensor"),
            P(("groups", "expert"), None),
            P(("groups", "expert"), None),
            P(None, ("expert", "tensor")),
            P(None, ("expert", "tensor")),
            P(("expert", "tensor"), None),
        ),
        out_specs=P(("groups", "expert"), "tensor"),
        check_vma=False,
    )
```

```python
import functools

import jax
import jax.numpy as jnp
from jax import lax
from jax.experimental import pallas as pl
from jax.experimental.pallas import tpu as pltpu
from jax.sharding import PartitionSpec as P

E_W = 4
SLOT = 10
SLAB = 16
FETCH = 2
OWN = 4
DOWNS = 2
TILE = 512
WIDE = 512
MICRO = 1_150_000_000
MIB = 1 << 20
VMEM = pltpu.VMEM
HBM = pltpu.HBM
DMA = pltpu.SemaphoreType.DMA


def spec(space):
    return pl.BlockSpec(memory_space=space)


def limit(mib):
    return pltpu.CompilerParams(vmem_limit_bytes=mib * MIB)


def lasts(micros):
    return pl.CostEstimate(flops=int(micros * MICRO), bytes_accessed=0, transcendentals=0)


def dot(a, b):
    return lax.dot_general(a, b, (((1,), (0,)), ((), ())), preferred_element_type=jnp.float32)


def folds(width):
    return 4 if width % 512 == 0 else 1


def slab_rows(width):
    return max(SLAB, folds(width) * SLOT)


def stack(slabs):
    return jnp.concatenate([ref[...].astype(jnp.float32) for ref in slabs], 0).astype(jnp.bfloat16)


def pieces(width):
    size = width // folds(width)
    return [(p, slice(p * size, (p + 1) * size)) for p in range(folds(width))]


def order(n):
    return [0, *range(2, n), 1]


def iota(shape, dim):
    return lax.broadcasted_iota(jnp.int32, shape, dim)


def job_copies(jobs, half, up_hbm, targets, sems):
    q = lax.axis_index("tensor")
    copies = []
    for i, job in enumerate(jobs):
        start = (q ^ (job // 2)) * 2 * half + (job % 2) * half
        at = pl.ds(pl.multiple_of(start, 128), half)
        copies.append(pltpu.make_async_copy(up_hbm.at[at, :], targets[i], sems.at[i]))
    return copies


def select_kernel(n, ids_hbm, route_hbm, tok_hbm, comb_ref, *refs):
    slabs, (ids_ref, route_ref, tok_ref, sems) = refs[:n], refs[n:]
    inputs = [
        pltpu.make_async_copy(source, target, sems.at[i])
        for i, (source, target) in enumerate(
            ((ids_hbm, ids_ref), (route_hbm, route_ref), (tok_hbm, tok_ref))
        )
    ]
    for copy in inputs:
        copy.start()
    for copy in inputs:
        copy.wait()
    me = lax.axis_index("expert")
    replicas = n // E_W
    ids, route, tok = ids_ref[...], route_ref[...], tok_ref[...]
    count = tok.shape[0]
    before = (iota((count, count), 0) <= iota((count, count), 1)).astype(jnp.bfloat16)
    slot = iota((SLAB, count), 0).astype(jnp.float32)
    width = tok.shape[1]
    tall = slab_rows(width)
    row = iota((tall, count), 0).astype(jnp.float32)
    members, positions = [], []
    for k in range(n):
        hit = ids == (me ^ k) // replicas
        member = jnp.sum(jnp.where(hit, 1.0, 0.0), axis=0, keepdims=True)
        weight = jnp.sum(jnp.where(hit, route, 0.0), axis=0, keepdims=True)
        member = jnp.broadcast_to(member, (SLAB, count))
        position = dot(member.astype(jnp.bfloat16), before) - 1.0
        placed = jnp.where(position == slot, member, 0.0)
        comb_ref[k * SLAB : (k + 1) * SLAB, :] = placed * weight
        members.append(jnp.broadcast_to(member[:1], (tall, count)))
        positions.append(jnp.broadcast_to(position[:1], (tall, count)))
    total = None
    for p, piece in pieces(width):
        take = [
            jnp.where(position + float(p * SLOT) == row, member, 0.0)
            for position, member in zip(positions, members)
        ]
        part = dot(jnp.concatenate(take, 0).astype(jnp.bfloat16), tok[:, piece])
        total = part if total is None else total + part
    for k in range(n):
        slabs[k][...] = total[k * tall : (k + 1) * tall].astype(jnp.bfloat16)


def select(n, ids, route, tokens):
    count, width = tokens.shape
    out = pl.pallas_call(
        functools.partial(select_kernel, n),
        out_shape=[VMEM((n * SLAB, count), jnp.float32)]
        + [VMEM((slab_rows(width), width // folds(width)), jnp.bfloat16)] * n,
        in_specs=[spec(HBM)] * 3,
        out_specs=[spec(VMEM)] * (n + 1),
        scratch_shapes=[
            VMEM(ids.shape, ids.dtype),
            VMEM(route.shape, route.dtype),
            VMEM(tokens.shape, tokens.dtype),
            DMA((3,)),
        ],
        compiler_params=limit(4),
        cost_estimate=lasts(40),
        name="select",
    )(ids, route, tokens)
    return out[0], out[1:]


def compact_kernel(n, *refs):
    slabs, rows_ref = refs[:n], refs[-1]
    full = stack(slabs)
    tall, width = slabs[0].shape[0], rows_ref.shape[1]
    col = iota((n * SLOT, n * tall), 1)
    for p, piece in pieces(width):
        s = col % tall - p * SLOT
        take = (iota((n * SLOT, n * tall), 0) == col // tall * SLOT + s) & (s >= 0) & (s < SLOT)
        rows_ref[:, piece] = dot(take.astype(jnp.bfloat16), full).astype(jnp.bfloat16)


def compact(width, slabs, after):
    n = len(slabs)
    return pl.pallas_call(
        functools.partial(compact_kernel, n),
        out_shape=VMEM((n * SLOT, width), jnp.bfloat16),
        in_specs=[spec(VMEM)] * (n + 1),
        out_specs=spec(VMEM),
        compiler_params=limit(4),
        name="compact",
    )(*slabs, after)


def chunk(weight_ref, k, width, side, half, tile):
    start = (lax.axis_index("tensor") ^ k) * width + side
    return weight_ref[pl.ds(pl.multiple_of(start, 128), half), tile]


def tiles(n):
    return [slice(at, at + min(TILE, n)) for at in range(0, n, min(TILE, n))]


def fetch_kernel(jobs, half, order_ref, up_hbm, *refs):
    held, sems = refs[:-1], refs[-1]
    copies = job_copies(jobs, half, up_hbm, held, sems)
    for copy in copies:
        copy.start()
    for copy in copies:
        copy.wait()


def fetch(jobs, half, order, w_up):
    shape = (half, w_up.shape[1])
    return pl.pallas_call(
        functools.partial(fetch_kernel, jobs, half),
        out_shape=[VMEM(shape, jnp.bfloat16)] * len(jobs),
        in_specs=[spec(VMEM), spec(HBM)],
        out_specs=[spec(VMEM)] * len(jobs),
        scratch_shapes=[DMA((len(jobs),))],
        compiler_params=limit(2),
        cost_estimate=lasts(0.2),
        name="fetch",
    )(order, w_up)


def own_kernel(jobs, n, rows_ref, comb_ref, up_low, up_high, up_hbm, sum_u, mix_ref, *refs):
    held, sems = refs[:-1], refs[-1]
    half = rows_ref.shape[1] // 2
    copies = job_copies(jobs, half, up_hbm, held, sems)
    for copy in copies:
        copy.start()
    low, high = rows_ref[:, :half], rows_ref[:, half:]
    steps = tiles(sum_u.shape[1])
    done = 0
    for i, tile in enumerate(steps):
        sum_u[:, tile] = dot(low, up_low[:, tile]) + dot(high, up_high[:, tile])
        while done < len(copies) and done * len(steps) < (i + 1) * len(copies):
            copies[done].wait()
            done += 1
    comb = comb_ref[...].T
    count, width = comb.shape[0], rows_ref.shape[1]
    tall = slab_rows(width)
    row, col = iota((n * SLAB, n * tall), 0), iota((n * SLAB, n * tall), 1)
    for i in range(3):
        term = comb.astype(jnp.bfloat16)
        comb = comb - term.astype(jnp.float32)
        for p, _ in pieces(width):
            s = col % tall - p * SLOT
            take = (row == col // tall * SLAB + s) & (s >= 0) & (s < SLOT)
            part = dot(term, take.astype(jnp.bfloat16)).astype(jnp.bfloat16)
            mix_ref[i, p * count : (p + 1) * count, :] = part
    for copy in copies[done:]:
        copy.wait()


def own(jobs, axis, rows, comb, held, w_up):
    (m, width), n = rows.shape, w_up.shape[1]
    mix = (3, folds(width) * comb.shape[1], axis * slab_rows(width))
    return pl.pallas_call(
        functools.partial(own_kernel, jobs, axis),
        out_shape=[VMEM((m, n), jnp.float32), VMEM(mix, jnp.bfloat16)]
        + [VMEM((width // 2, n), jnp.bfloat16)] * len(jobs),
        in_specs=[spec(VMEM)] * 4 + [spec(HBM)],
        out_specs=[spec(VMEM)] * (2 + len(jobs)),
        scratch_shapes=[DMA((len(jobs),))],
        compiler_params=limit(2),
        cost_estimate=lasts(0.2),
        name="own",
    )(rows, comb, *held, w_up)


def second_kernel(rows_ref, sum_u, up_low, up_high, out_ref):
    half = rows_ref.shape[1] // 2
    for tile in tiles(sum_u.shape[1]):
        part = dot(rows_ref[:, :half], up_low[:, tile]) + dot(rows_ref[:, half:], up_high[:, tile])
        out_ref[:, tile] = sum_u[:, tile] + part


def second(rows, sum_u, held):
    return pl.pallas_call(
        second_kernel,
        out_shape=VMEM(sum_u.shape, jnp.float32),
        in_specs=[spec(VMEM)] * 4,
        out_specs=spec(VMEM),
        compiler_params=limit(2),
        cost_estimate=lasts(1),
        name="second",
    )(rows, sum_u, *held)


def down_copy(k, down_hbm, target, sem):
    width = target.shape[1]
    q = lax.axis_index("tensor")
    at = pl.ds(pl.multiple_of((q ^ k) * width, 128), width)
    return pltpu.make_async_copy(down_hbm.at[:, at], target, sem)


def rest_kernel(outs, first, *refs):
    parts = len(outs) + 3
    rows, refs = refs[:parts], refs[parts:]
    held, refs = refs[: first - 4], refs[first - 4 :]
    start_u, gate_ref, up_hbm, down_hbm, hidden_ref, next_ref = refs[:6]
    sent, refs = refs[6 : 6 + len(outs)], refs[6 + len(outs) :]
    late, down2, sum_g, late_sems, down_sems, next_sem = refs
    width = rows[0].shape[1]
    half = width // 2
    slots, deep = down2.shape[:2]
    n = hidden_ref.shape[1]
    wide = min(WIDE, n)
    deep_gate = 256 if width % 256 == 0 else 128
    cuts = n // deep
    jobs = range(first, 2 * parts)
    lates = job_copies(jobs, half, up_hbm, [late.at[i] for i in range(len(jobs))], late_sems)
    downs = []
    for i in range(cuts * len(outs)):
        rows_at, slot = down_hbm.at[pl.ds(i % cuts * deep, deep), :], i % slots
        downs.append(down_copy(outs[i // cuts], rows_at, down2.at[slot], down_sems.at[slot]))
    for copy in lates:
        copy.start()
    ups = list(held) + [late.at[i] for i in range(len(jobs))]

    def gate_part(step):
        at = pl.ds(pl.multiple_of(step * wide, 128), wide)
        total = None
        for k in range(parts):
            for side in range(0, width, deep_gate):
                row = rows[k][:, side : side + deep_gate]
                part = dot(row, chunk(gate_ref, k, width, side, deep_gate, at))
                total = part if total is None else total + part
        sum_g[:, at] = total

    middle = n // wide // 2
    pl.loop(0, middle)(gate_part)
    after = down_copy(2, down_hbm, next_ref, next_sem)
    for copy in [*downs[:slots], after]:
        copy.start()
    pl.loop(middle, n // wide)(gate_part)
    for copy in lates:
        copy.wait()

    @pl.loop(0, n // wide)
    def _(step):
        at = pl.ds(pl.multiple_of(step * wide, 128), wide)
        total = start_u[:, at]
        for k in range(2, parts):
            total += dot(rows[k][:, :half], ups[2 * k - 4][:, at])
            total += dot(rows[k][:, half:], ups[2 * k - 3][:, at])
        gate = sum_g[:, at]
        hidden_ref[:, at] = (gate / (1.0 + jnp.exp(-gate)) * total).astype(jnp.bfloat16)

    for i in range(len(outs)):
        for j in range(cuts):
            piece = cuts * i + j
            downs[piece].wait()

            @pl.loop(0, 2)
            def _(step):
                at = pl.ds(pl.multiple_of(step * half, 128), half)
                mid = hidden_ref[:, j * deep : (j + 1) * deep]
                part = dot(mid, down2[piece % slots, :, at])
                if j > 0:
                    part += sum_g[:, at]
                if j < cuts - 1:
                    sum_g[:, at] = part
                else:
                    sent[i][:, at] = part.astype(jnp.bfloat16)

            if piece + slots < len(downs):
                downs[piece + slots].start()
    after.wait()


def rest(outs, rows, held, sum_u, w_gate, w_up, w_down):
    m, n = sum_u.shape
    width = rows[0].shape[1]
    cuts = 2 if n % 256 == 0 else 1
    first = 4 + len(held)
    late = max(1, 2 * len(rows) - first)
    return pl.pallas_call(
        functools.partial(rest_kernel, outs, first),
        out_shape=[VMEM((m, n), jnp.bfloat16), VMEM((n, width), jnp.bfloat16)]
        + [VMEM((m, width), jnp.bfloat16)] * len(outs),
        in_specs=[spec(VMEM)] * (len(rows) + len(held) + 2) + [spec(HBM)] * 2,
        out_specs=[spec(VMEM)] * (2 + len(outs)),
        scratch_shapes=[
            VMEM((late, width // 2, n), jnp.bfloat16),
            VMEM((DOWNS, n // cuts, width), jnp.bfloat16),
            VMEM((m, max(n, width)), jnp.float32),
            DMA((late,)),
            DMA((DOWNS,)),
            DMA,
        ],
        compiler_params=limit(20),
        cost_estimate=lasts(10),
        name="rest",
    )(*rows, *held, sum_u, w_gate, w_up, w_down)


def pass_kernel(k, hidden_ref, weight_ref, down_hbm, sent, next_ref, sem):
    copy = down_copy(k, down_hbm, next_ref, sem)
    copy.start()
    half = sent.shape[1] // 2

    @pl.loop(0, 2)
    def _(step):
        at = pl.ds(pl.multiple_of(step * half, 128), half)
        sent[:, at] = dot(hidden_ref[...], weight_ref[:, at]).astype(jnp.bfloat16)

    copy.wait()


def pass_on(k, hidden, weight, w_down):
    shape = (hidden.shape[0], weight.shape[1])
    return pl.pallas_call(
        functools.partial(pass_kernel, k),
        out_shape=[VMEM(shape, jnp.bfloat16), VMEM(weight.shape, jnp.bfloat16)],
        in_specs=[spec(VMEM)] * 2 + [spec(HBM)],
        out_specs=[spec(VMEM)] * 2,
        scratch_shapes=[DMA],
        compiler_params=limit(8),
        cost_estimate=lasts(3),
        name="pass_on",
    )(hidden, weight, w_down)


def keep_kernel(hidden_ref, weight_ref, *refs):
    terms, total_ref = refs[:-1], refs[-1]
    total = dot(hidden_ref[...], weight_ref[...])
    for term in terms:
        total = total + term[...].astype(jnp.float32)
    total_ref[...] = total


def keep(hidden, weight, terms):
    m, width = hidden.shape[0], weight.shape[1]
    return pl.pallas_call(
        keep_kernel,
        out_shape=VMEM((m, width), jnp.float32),
        in_specs=[spec(VMEM)] * (2 + len(terms)),
        out_specs=spec(VMEM),
        compiler_params=limit(4),
        cost_estimate=lasts(1),
        name="keep",
    )(hidden, weight, *terms)


def gather_kernel(total_ref, *refs):
    terms, sum_ref = refs[:-1], refs[-1]
    total = total_ref[...]
    for term in terms:
        total = total + term[...].astype(jnp.float32)
    sum_ref[...] = total


def gather(total, terms):
    return pl.pallas_call(
        gather_kernel,
        out_shape=VMEM(total.shape, jnp.float32),
        in_specs=[spec(VMEM)] * (1 + len(terms)),
        out_specs=spec(VMEM),
        compiler_params=limit(4),
        cost_estimate=lasts(2),
        name="gather",
    )(total, *terms)


def add_kernel(n, total_ref, *refs):
    terms, slabs = refs[:-n], refs[-n:]
    total = total_ref[...]
    for term in terms:
        total = total + term[...].astype(jnp.float32)
    total = total.astype(jnp.bfloat16)
    width = total.shape[1]
    tall = slab_rows(width)
    row, col = iota((n * tall, n * SLOT), 0), iota((n * tall, n * SLOT), 1)
    full = None
    for p, piece in pieces(width):
        s = row % tall - p * SLOT
        take = (col == row // tall * SLOT + s) & (s >= 0) & (s < SLOT)
        part = dot(take.astype(jnp.bfloat16), total[:, piece])
        full = part if full is None else full + part
    for slab, k in zip(slabs, order(n)):
        slab[...] = full[k * tall : (k + 1) * tall].astype(jnp.bfloat16)


def add(n, total, terms):
    width = total.shape[1]
    return pl.pallas_call(
        functools.partial(add_kernel, n),
        out_shape=[VMEM((slab_rows(width), width // folds(width)), jnp.bfloat16)] * n,
        in_specs=[spec(VMEM)] * (1 + len(terms)),
        out_specs=[spec(VMEM)] * n,
        compiler_params=limit(4),
        name="add",
    )(total, *terms)


def combine_kernel(mix_ref, *refs):
    slabs, out_ref = refs[:-1], refs[-1]
    full = stack([slab for _, slab in sorted(zip(order(len(slabs)), slabs), key=lambda x: x[0])])
    count, width = out_ref.shape
    total = dot(mix_ref[0], full) + (dot(mix_ref[1], full) + dot(mix_ref[2], full))
    for p, piece in pieces(width):
        out_ref[:, piece] = total[p * count : (p + 1) * count].astype(jnp.bfloat16)


def combine(width, mix, slabs):
    n = len(slabs)
    return pl.pallas_call(
        combine_kernel,
        out_shape=jax.ShapeDtypeStruct((mix.shape[1] // folds(width), width), jnp.bfloat16),
        in_specs=[spec(VMEM)] * (n + 1),
        out_specs=spec(VMEM),
        compiler_params=limit(4),
        name="combine",
    )(mix, *slabs)


def swap(x, axis, k):
    size = lax.axis_size(axis)
    return lax.ppermute(x, axis, [(i, i ^ k) for i in range(size)])


def per_device(*args):
    tokens, ids, route, w_up, w_down = (
        pltpu.with_memory_space_constraint(x, HBM)
        for x in (args[0], args[1].T, args[2].T, args[4], args[5])
    )
    w_gate = args[3]
    n, parts = lax.axis_size("expert"), lax.axis_size("tensor")
    width = tokens.shape[1]
    comb, slabs = select(n, ids, route, tokens)
    slabs = [slabs[0]] + [swap(slabs[k], "expert", k) for k in range(1, n)]
    held = fetch(range(FETCH), width // 2, comb, w_up)
    mine = compact(width, slabs, held[-1])
    rows = [mine] + [swap(mine, "tensor", k) for k in range(1, parts)]
    sum_u, mix, *more = own(range(FETCH, OWN), n, mine, comb, held[:2], w_up)
    held = [*held[2:], *more]
    sum_u = second(rows[1], sum_u, held[:2])
    held = held[2:]
    far = list(range(parts - 1, 2, -1))
    hidden, weight, *sent = rest(far, rows, held, sum_u, w_gate, w_up, w_down)
    terms = [swap(x, "tensor", k) for k, x in zip(far, sent)]
    sent, weight = pass_on(1, hidden, weight, w_down)
    late = swap(sent, "tensor", 2)
    sent, weight = pass_on(0, hidden, weight, w_down)
    last = swap(sent, "tensor", 1)
    total = gather(keep(hidden, weight, terms), [late])
    back = add(n, total, [last])
    back = [swap(x, "expert", k) if k else x for k, x in zip(order(n), back)]
    return combine(width, mix, back)


def solution(mesh):
    return jax.shard_map(
        per_device,
        mesh=mesh,
        in_specs=(
            P(("groups", "expert"), "tensor"),
            P(("groups", "expert"), None),
            P(("groups", "expert"), None),
            P(None, ("expert", "tensor")),
            P(None, ("expert", "tensor")),
            P(("expert", "tensor"), None),
        ),
        out_specs=P(("groups", "expert"), "tensor"),
        check_vma=False,
    )
```
